128 devices in a mesh: rows: 32 (over x, z, core), sub: 4 (over y).
Axes of the slice: x: 4, y: 4, z: 4, core: 2. Of those that a mesh axis runs over, the one named last changes fastest.
Arguments:
- vectors: bfloat16 [32768, 1024], P(('rows', 'sub')), may hold values from -6 to 6
- coarse_list: int32 [32768], P(('rows', 'sub')), may hold values from 0 to 524287, as said below
- list_slot: int32 [524288], replicated, may hold values from 0 to 524287, as said below
- codes: int32 [32768, 64], P(('rows', 'sub')), may hold values from 0 to 255
- centroids: bfloat16 [524288, 1024], P(('rows', 'sub')), may hold values from -3 to 3
- rotation: bfloat16 [1024, 1024], replicated, may hold values from -0.1875 to 0.1875
- codebook: bfloat16 [64, 256, 16], replicated, may hold values from -6 to 6
Outputs:
- new_codebook: float32 [64, 256, 16], P('sub', 'rows')
- procrustes: float32 [1024, 1024], P(('rows', 'sub'))
The draws below stay inside these ranges and needn't reach their ends.
Inputs may be any that keep to these rules, and one draw needn't show every extreme that they name: `list_slot`: a permutation. `coarse_list`: for slot s, the owning device is s // 4096 along rows+sub. Of the vectors of one device, at most 10 have lists owned by one device, and one device owns the lists of exactly 10 vectors of every device.
All inputs are finite; a program needn't handle non-finite values.
Results may differ from the reference program's by a relative error of at most 0.0042.
Values may be sent and summed in bfloat16 or wider, within the bound.
A program may use at most 128 MiB of HBM per device.

```python
import math
import jax
import jax.numpy as jnp
import numpy as np
from jax import lax

D = 1024
M = 64
K = 256
DS = 16
LIST_DEV = 4096
TOK_DEV = 256
LISTS = 524288
TOKENS = 32768
CAP = 10
DEVICES = 128


def routing(key):
    list_slot = jax.random.permutation(jax.random.fold_in(key, 101), LISTS).astype(jnp.int32)
    slot_list = jnp.argsort(list_slot).astype(jnp.int32)
    hot_owner = jax.random.randint(jax.random.fold_in(key, 102), (), 0, DEVICES)
    step_up = jax.random.randint(jax.random.fold_in(key, 103), (DEVICES,), 1, DEVICES)
    warm_owner = (hot_owner + step_up) % DEVICES
    warm_count = jax.random.randint(jax.random.fold_in(key, 104), (DEVICES,), 1, CAP + 1)
    offset = jax.random.randint(jax.random.fold_in(key, 105), (DEVICES,), 0, DEVICES - 2)
    position = jnp.arange(TOK_DEV, dtype=jnp.int32)
    leftover = position[None, :] - CAP - warm_count[:, None]
    other = (leftover + offset[:, None]) % (DEVICES - 2)
    lower_end = jnp.minimum(hot_owner, warm_owner)[:, None]
    upper_end = jnp.maximum(hot_owner, warm_owner)[:, None]
    other = other + (other >= lower_end).astype(jnp.int32)
    other = other + (other >= upper_end).astype(jnp.int32)
    destination = jnp.where(position[None, :] < CAP, hot_owner, jnp.where(leftover < 0, warm_owner[:, None], other))
    shuffle = jax.vmap(lambda key_row: jax.random.permutation(key_row, TOK_DEV))(jax.random.split(jax.random.fold_in(key, 106), DEVICES))
    destination = jnp.take_along_axis(destination, shuffle, axis=1)
    within = jax.random.randint(jax.random.fold_in(key, 107), (DEVICES, TOK_DEV), 0, LIST_DEV)
    slot_of = (destination * LIST_DEV + within).reshape(-1)
    return (list_slot, slot_list[slot_of].astype(jnp.int32))


def draw_list_slot(key, part):
    shared = routing(key)
    return shared[0]


def draw_coarse_list(key, part):
    shared = routing(key)
    return shared[1]


def set_ends(result, own_key, least, high):
    spot = [jax.random.randint(jax.random.fold_in(own_key, axis), (), 0, length) for axis, length in enumerate(result.shape)]
    longest = result.shape.index(max(result.shape))
    beside = spot[:longest] + [(spot[longest] + 1) % result.shape[longest]] + spot[longest + 1:]
    return result.at[tuple(spot)].set(least).at[tuple(beside)].set(high)


def block_levels(own_key, shape, cuts, least, largest):
    factor_of = 1.0
    for dim, shards_of in cuts:
        heights = jax.random.uniform(jax.random.fold_in(jax.random.fold_in(own_key, 6), dim), (shards_of,), jnp.float32, least / len(cuts), largest / len(cuts))
        factor_of = factor_of * jnp.repeat(jnp.exp(heights), shape[dim] // shards_of).reshape((-1,) + (1,) * (len(shape) - 1 - dim))
    return factor_of


def cumulative_ranks(number_of, slope):
    portions = [(1 << 20) // math.isqrt(grade ** slope) + 1 for grade in range(1, number_of + 1)]
    spread = 1 + sum(portions) // (1 << 30)
    return np.cumsum(np.array([max(1, weight // spread) for weight in portions]))


def skewed_ids(key, extent, count, skew):
    listing = cumulative_ranks(count, skew)
    ticket = jax.random.randint(jax.random.fold_in(key, 1), extent, 0, int(listing[count - 1]))
    rank = jnp.searchsorted(jnp.asarray(listing, jnp.int32), ticket, side="right")
    return jax.random.permutation(jax.random.fold_in(key, 2), count)[rank].astype(jnp.int32)


def normal_values(stream_key, extent, spread, reach, cuts=(), held_as=jnp.bfloat16):
    gain = block_levels(stream_key, extent, cuts, -0.22, 0.18) if cuts else 1.0
    drawn = jax.random.normal(stream_key, extent, jnp.float32) * spread * gain
    return jnp.minimum(jnp.maximum(drawn, -reach), reach).astype(held_as)


def setup_inputs(seed: int = 0) -> dict:
    splits = jax.random.split(jax.random.key(seed), 8)
    return {
        "vectors": normal_values(splits[0], (TOKENS, D), 1.0, 6.0, ((0, 128),)),
        "coarse_list": draw_coarse_list(jax.random.fold_in(splits[7], 71), 0),
        "list_slot": draw_list_slot(jax.random.fold_in(splits[7], 71), 0),
        "codes": set_ends(skewed_ids(splits[3], (TOKENS, M), K, 2), jax.random.fold_in(splits[3], 3), 0, K - 1).astype(jnp.int32),
        "centroids": normal_values(splits[4], (LISTS, D), 0.5, 3.0, ((0, 128),)),
        "rotation": normal_values(splits[5], (D, D), D ** -0.5, 0.1875),
        "codebook": normal_values(splits[6], (M, K, DS), 1.0, 6.0),
    }


def reference(vectors, coarse_list, list_slot, codes, centroids, rotation, codebook):
    slot_of = list_slot[coarse_list]
    residual = (vectors.astype(jnp.float32) - centroids[slot_of].astype(jnp.float32)).astype(jnp.bfloat16)
    rotated = jnp.dot(residual, rotation, preferred_element_type=jnp.float32).astype(jnp.bfloat16)

    def per_sub(sub_index):
        columns = lax.dynamic_slice_in_dim(rotated, sub_index * DS, DS, 1).astype(jnp.float32)
        code_ids = lax.dynamic_index_in_dim(codes, sub_index, 1, keepdims=False)
        code_total = jax.ops.segment_sum(columns, code_ids, K)
        counts = jax.ops.segment_sum(jnp.ones(code_ids.shape, jnp.float32), code_ids, K)
        centroid_table = lax.dynamic_index_in_dim(codebook, sub_index, 0, keepdims=False)
        rebuilt = centroid_table[code_ids]
        return (code_total / (counts[:, None] + 1.0), rebuilt)
    new_codebook, rebuilt = lax.map(per_sub, jnp.arange(M, dtype=jnp.int32))
    rebuilt = jnp.transpose(rebuilt, (1, 0, 2)).reshape(TOKENS, D)
    procrustes = jnp.dot(residual.T, rebuilt, preferred_element_type=jnp.float32) / jnp.sqrt(jnp.float32(TOKENS))
    return (new_codebook, procrustes)
```

```python
import jax
import jax.numpy as jnp
from jax import lax
from jax.experimental import pallas as pl
from jax.experimental.pallas import tpu as pltpu
from jax.sharding import PartitionSpec as P

D = 1024
M = 64
K = 256
DS = 16
CAP = 10
SLOT = 16
WIDE = D + 2 * 128 + 128
F32 = jnp.float32
BF = jnp.bfloat16
MESH = pl.DeviceIdType.MESH
VMEM = pltpu.VMEM

PARTS = ((0, 512, "xyz"), (512, 1024, "yzx"), (1024, WIDE, "zxy"))
DIM = {"x": 0, "z": 1, "y": 2}


def local_kernel(v_ref, c_ref, rotation_ref, codes_ref, table_ref, sums_ref, x_ref, reb_ref, hi_ref, lo_ref):
    near = v_ref.shape[0]
    tokens = x_ref.shape[0]
    blocks = tokens // 256
    x_ref[0:near, :] = v_ref[...]
    x_ref[near:tokens, :] = -c_ref[...]

    def decode(m, carry):
        row = codes_ref[pl.ds(m, 1), :]
        for block in range(tokens // 128):
            index = jnp.broadcast_to(row[:, block * 128 : (block + 1) * 128], (8, 128))
            low = index & 127
            halves = []
            for half in range(2):
                start = pl.multiple_of(m * DS + 8 * half, 8)
                first = jnp.take_along_axis(table_ref[pl.ds(start, 8), 0:128], low, axis=1)
                second = jnp.take_along_axis(table_ref[pl.ds(start, 8), 128:256], low, axis=1)
                halves.append(jnp.where(index >= 0, jnp.where(index >= 128, second, first), 0.0))
            reb_ref[pl.ds(pl.multiple_of(m * DS, DS), DS), block * 128 : (block + 1) * 128] = jnp.concatenate(
                halves, 0
            ).astype(BF)
        return carry

    lax.fori_loop(0, M, decode, 0)

    def rotate(i, carry):
        columns = pl.ds(pl.multiple_of(i * 256, 256), 256)
        turned = jnp.dot(x_ref[...], rotation_ref[:, columns], preferred_element_type=F32)
        upper = turned.astype(BF)
        hi_ref[:, columns] = upper
        lo_ref[:, columns] = (turned - upper.astype(F32)).astype(BF)
        return carry

    lax.fori_loop(0, D // 256, rotate, 0)

    def cross(i, carry):
        rows = pl.ds(pl.multiple_of(i * 256, 256), 256)
        block = lax.dot_general(
            x_ref[:, rows], reb_ref[...], (((0,), (1,)), ((), ())), preferred_element_type=F32
        )
        sums_ref[pl.ds(i * 4, 4), :, :, :, 0:D] = block.reshape(4, 2, 4, 8, D)
        return carry

    lax.fori_loop(0, D // 256, cross, 0)

    lane = lax.broadcasted_iota(jnp.int32, (256, 128), 1)
    level = lax.broadcasted_iota(jnp.int32, (K, 256), 0).astype(F32).astype(BF)
    one, zero = jnp.asarray(1, BF), jnp.asarray(0, BF)

    def totals(y, carry):
        counts = jnp.zeros((K, 128), F32)
        for g in range(2):
            columns = pl.ds(pl.multiple_of(y * 256 + g * 128, 128), 128)
            acc = jnp.zeros((K, 256), F32)
            for block in range(blocks):
                span = slice(block * 256, (block + 1) * 256)
                upper, lower = hi_ref[span, columns], lo_ref[span, columns]
                for j in range(8):
                    row = codes_ref[pl.ds(y * 16 + g * 8 + j, 1), span].astype(F32).astype(BF)
                    onehot = jnp.where(row == level, one, zero)
                    mine = lane // DS == j
                    right = jnp.concatenate([jnp.where(mine, upper, zero), jnp.where(mine, lower, zero)], 1)
                    acc = acc + jnp.dot(onehot, right, preferred_element_type=F32)
                    if block * 256 < near:
                        pick = jnp.where(lane == g * 8 + j, one, zero)
                        counts = counts + jnp.dot(onehot, pick, preferred_element_type=F32)
            both = acc[:, :128] + acc[:, 128:]
            sums_ref[:, :, pl.ds(y, 1), :, D + g * 128 : D + (g + 1) * 128] = both.reshape(16, 2, 1, 8, 128)
        sums_ref[:, :, pl.ds(y, 1), :, D + 256 : D + 384] = counts.reshape(16, 2, 1, 8, 128)
        return carry

    lax.fori_loop(0, 4, totals, 0)


def local_sums(vectors, fetched, rotation, codes_t, table):
    tokens = vectors.shape[0] + fetched.shape[0]
    return pl.pallas_call(
        local_kernel,
        out_shape=jax.ShapeDtypeStruct((16, 2, 4, 8, WIDE), F32),
        in_specs=[pl.BlockSpec(memory_space=VMEM)] * 5,
        out_specs=pl.BlockSpec(memory_space=VMEM),
        scratch_shapes=[
            VMEM((tokens, D), BF),
            VMEM((D, tokens), BF),
            VMEM((tokens, D), BF),
            VMEM((tokens, D), BF),
        ],
        compiler_params=pltpu.CompilerParams(vmem_limit_bytes=56 * 2**20),
        name="local_sums",
    )(vectors, fetched, rotation, codes_t, table)


def scatter_kernel(*refs):
    sums_ref, out_ref = refs[:2]
    scratch = refs[2:]
    pair_send, pair_recv, axis_send, axis_recv = scratch[-4:]
    buffers = [scratch[p * 6 : (p + 1) * 6] for p in range(3)]
    r, y = lax.axis_index("rows"), lax.axis_index("sub")
    core, z, x = r % 2, (r // 2) % 4, r // 8
    at = {"x": x, "y": y, "z": z}

    def device(axis, value):
        if axis == "x":
            return (r + (value - x) * 8, y)
        if axis == "z":
            return (r + (value - z) * 2, y)
        return (r, value)

    mate = (r + 1 - 2 * core, y)
    barrier = pltpu.get_barrier_semaphore()
    pl.semaphore_signal(barrier, inc=1, device_id=mate, device_id_type=MESH)
    for axis in "xyz":
        for step in range(1, 4):
            pl.semaphore_signal(
                barrier, inc=1, device_id=device(axis, (at[axis] + step) % 4), device_id_type=MESH
            )
    pl.semaphore_wait(barrier, 10)

    pair = []
    for p, (begin, end, order) in enumerate(PARTS):
        copy = pltpu.make_async_remote_copy(
            src_ref=sums_ref.at[:, 1 - core, :, :, begin:end],
            dst_ref=buffers[p][0],
            send_sem=pair_send.at[p],
            recv_sem=pair_recv.at[p],
            device_id=mate,
            device_id_type=MESH,
        )
        copy.start()
        pair.append(copy)

    def view(ref, dims, axis, index):
        place = tuple(index if d == axis else slice(None) for d in dims)
        return ref.at[place]

    def send(p, stage, source, target, dims, axis):
        copies = []
        for step in range(1, 4):
            peer = (at[axis] + step) % 4
            copy = pltpu.make_async_remote_copy(
                src_ref=view(source, dims, axis, peer),
                dst_ref=target.at[step - 1],
                send_sem=axis_send.at[p, stage, step - 1],
                recv_sem=axis_recv.at[p, stage, step - 1],
                device_id=device(axis, peer),
                device_id_type=MESH,
            )
            copy.start()
            copies.append(copy)
        return copies

    moving = [None] * 3
    for p, (begin, end, order) in enumerate(PARTS):
        got, first = buffers[p][0], buffers[p][1]
        pair[p].wait_recv()

        def add(i, carry, got=got, first=first, begin=begin, end=end):
            first[i // 4, i % 4] = sums_ref[i, core, :, :, begin:end] + got[i]
            return carry

        lax.fori_loop(0, 16, add, 0)
        moving[p] = send(p, 0, first, buffers[p][2], "xzy", order[0])
    sent = []
    for stage in range(1, 4):
        for p, (begin, end, order) in enumerate(PARTS):
            axis = order[stage - 1]
            dims = "".join(d for d in "xzy" if d not in order[: stage - 1])
            rest = dims.replace(axis, "")
            source = (buffers[p][1], buffers[p][3], buffers[p][5])[stage - 1]
            target = (buffers[p][2], buffers[p][4], None)[stage - 1]
            for copy in moving[p]:
                copy.wait_recv()
            sent += moving[p]
            if stage < 3:
                following = (buffers[p][3], buffers[p][5])[stage - 1]
                following[...] = (
                    view(source, dims, axis, at[axis])[...] + target[0] + target[1] + target[2]
                )
                nxt = buffers[p][4] if stage == 1 else last_of(scratch, p)
                moving[p] = send(p, stage, following, nxt, rest, order[stage])
            else:
                landed = last_of(scratch, p)
                out_ref[:, begin:end] = source[at[axis]] + landed[0] + landed[1] + landed[2]
    for copy in pair + sent:
        copy.wait_send()


def last_of(scratch, p):
    return scratch[18 + p]


def scatter_sums(sums):
    scratch = []
    for begin, end, order in PARTS:
        wide = end - begin
        scratch += [
            VMEM((16, 4, 8, wide), F32),
            VMEM((4, 4, 4, 8, wide), F32),
            VMEM((3, 4, 4, 8, wide), F32),
            VMEM((4, 4, 8, wide), F32),
            VMEM((3, 4, 8, wide), F32),
            VMEM((4, 8, wide), F32),
        ]
    for begin, end, order in PARTS:
        scratch.append(VMEM((3, 8, end - begin), F32))
    return pl.pallas_call(
        scatter_kernel,
        out_shape=jax.ShapeDtypeStruct((8, WIDE), F32),
        in_specs=[pl.BlockSpec(memory_space=VMEM)],
        out_specs=pl.BlockSpec(memory_space=VMEM),
        scratch_shapes=scratch
        + [
            pltpu.SemaphoreType.DMA((3,)),
            pltpu.SemaphoreType.DMA((3,)),
            pltpu.SemaphoreType.DMA((3, 3, 3)),
            pltpu.SemaphoreType.DMA((3, 3, 3)),
        ],
        compiler_params=pltpu.CompilerParams(
            collective_id=0, has_side_effects=True, vmem_limit_bytes=56 * 2**20
        ),
        name="scatter_sums",
    )(sums)


def per_device(vectors, coarse_list, list_slot, codes, centroids, rotation, codebook):
    devices = lax.axis_size(("rows", "sub"))
    near = vectors.shape[0]
    list_rows = centroids.shape[0]
    slot_of = list_slot[coarse_list]
    owner_of = slot_of // list_rows
    local_row = slot_of % list_rows
    earlier = jnp.arange(near)[:, None] < jnp.arange(near)[None, :]
    rank = jnp.sum((owner_of[:, None] == owner_of[None, :]) & earlier, axis=0)
    position = owner_of * SLOT + rank
    message = jnp.concatenate(
        [codes + 1, (local_row // 64 + 1)[:, None], (local_row % 64 + 1)[:, None], jnp.zeros((near, 62), jnp.int32)],
        axis=1,
    ).astype(BF)
    place = (jnp.arange(devices * SLOT)[:, None] == position[None, :]).astype(BF)
    outgoing = jnp.dot(place, message, preferred_element_type=F32).astype(BF)
    incoming = lax.all_to_all(
        outgoing.reshape(devices, SLOT, 128), ("rows", "sub"), split_axis=0, concat_axis=0, tiled=True
    )
    arrived = incoming[:, :CAP, :].astype(jnp.int32).transpose(2, 1, 0).reshape(128, CAP * devices) - 1
    row = arrived[M] * 64 + arrived[M + 1]
    fetched = centroids[jnp.maximum(row, 0)]
    codes_t = jnp.concatenate([codes.T, arrived[:M]], axis=1)
    table = codebook.transpose(0, 2, 1).reshape(D, K).astype(F32)
    summed = scatter_sums(local_sums(vectors, fetched, rotation, codes_t, table))
    procrustes = summed[:, :D] / jnp.sqrt(jnp.float32(near * devices))
    code_total = summed[:, D : D + 256].reshape(8, 16, DS).transpose(1, 0, 2)
    counts = summed[:, D + 256 : D + 272].T
    return (code_total / (counts[:, :, None] + 1.0), procrustes)


def solution(mesh):
    placed = (
        P(("rows", "sub"), None),
        P(("rows", "sub")),
        P(),
        P(("rows", "sub"), None),
        P(("rows", "sub"), None),
        P(),
        P(),
    )
    return jax.shard_map(
        per_device,
        mesh=mesh,
        in_specs=placed,
        out_specs=(P("sub", "rows", None), P(("rows", "sub"), None)),
        check_vma=False,
    )
```

```python
import jax
import jax.numpy as jnp
from jax import lax
from jax.experimental import pallas as pl
from jax.experimental.pallas import tpu as pltpu
from jax.sharding import PartitionSpec as P

D = 1024
M = 64
K = 256
DS = 16
NEAR = 256
LISTS = 4096
DEVICES = 128
CAP = 10
SLOT = 16
FAR = CAP * DEVICES
CHUNK = 512
F32 = jnp.float32
BF = jnp.bfloat16
I32 = jnp.int32
MESH = pl.DeviceIdType.MESH
VMEM = pltpu.VMEM
ANY = pl.ANY
DMA = pltpu.SemaphoreType.DMA

PARTS = ((0, 384, "x", "zy"), (384, 768, "y", "xz"), (768, 1024, "z", "xy"))
DIMS = "xzy"
NT = (((1,), (1,)), ((), ()))
TT = (((0,), (1,)), ((), ()))


def onehot(row, level):
    return jnp.where(row == level, jnp.asarray(1, BF), jnp.asarray(0, BF))


def iota(shape, dim):
    return lax.broadcasted_iota(I32, shape, dim)


def levels(count, width):
    return iota((count, width), 0).astype(F32).astype(BF)


def drain(ref, semaphore):
    pltpu.make_async_copy(ref, ref, semaphore).wait()


def kernel(
    slot_ref,
    codes_ref,
    book_ref,
    vectors_hbm,
    rotation_hbm,
    centroids_hbm,
    out_book_ref,
    out_cross_ref,
    vectors_ref,
    rotation_ref,
    chunk_ref,
    table_ref,
    wide_ref,
    table_book_ref,
    message_ref,
    arrived_ref,
    arrived_wide_ref,
    near_codes_ref,
    far_codes_ref,
    row_ref,
    row_smem,
    counts_ref,
    near_reb_ref,
    far_reb_ref,
    stage_ref,
    far_x_ref,
    turned_ref,
    cross_ref,
    total_ref,
    cross_half_ref,
    ring_refs,
    cross_plane_ref,
    cross_got_ref,
    total_half_ref,
    total_side_ref,
    total_plane_ref,
    total_got_ref,
    local_sem,
    chunk_sem,
    message_send,
    message_recv,
    cross_core_send,
    cross_core_recv,
    ring_send,
    ring_recv,
    cross_plane_send,
    cross_plane_recv,
    total_core_send,
    total_core_recv,
    total_side_send,
    total_side_recv,
    total_plane_send,
    total_plane_recv,
):
    r, y = lax.axis_index("rows"), lax.axis_index("sub")
    core, z, x = r % 2, (r // 2) % 4, r // 8
    me = r * 4 + y
    at = {"x": x, "y": y, "z": z}

    def device(**place):
        spot = dict(at, **place)
        return ((spot["x"] * 4 + spot["z"]) * 2 + core, spot["y"])

    mate = (r + 1 - 2 * core, y)

    def remote(source, target, send, recv, to):
        return pltpu.make_async_remote_copy(
            src_ref=source, dst_ref=target, send_sem=send, recv_sem=recv, device_id=to, device_id_type=MESH
        )

    barrier = pltpu.get_barrier_semaphore()

    def greet(step, carry):
        other = (me + step) % DEVICES
        pl.semaphore_signal(barrier, inc=1, device_id=(other // 4, other % 4), device_id_type=MESH)
        return carry

    lax.fori_loop(1, DEVICES, greet, 0)

    loads = [
        pltpu.make_async_copy(vectors_hbm, vectors_ref, local_sem.at[0]),
        pltpu.make_async_copy(rotation_hbm, rotation_ref, local_sem.at[1]),
    ]
    for load in loads:
        load.start()

    def chunk_load(i):
        return pltpu.make_async_copy(
            centroids_hbm.at[pl.ds(i * CHUNK, CHUNK)], chunk_ref.at[i % 2], chunk_sem.at[i % 2]
        )

    chunk_load(0).start()
    chunk_load(1).start()

    along = jnp.broadcast_to(slot_ref[...].astype(F32), (NEAR, NEAR))
    down = along.T.astype(I32)
    along = along.astype(I32)
    owner = along // LISTS
    same = (owner == down // LISTS) & (iota((NEAR, NEAR), 0) < iota((NEAR, NEAR), 1))
    rank = jnp.sum(jnp.where(same, 1, 0), axis=0, keepdims=True)
    position = owner[0:1] * SLOT + rank
    wide_ref[...] = jnp.zeros((NEAR, 128), F32)
    wide_ref[:, 0:M] = (codes_ref[...] + 1).astype(F32)
    local_row = down[:, 0:128] % LISTS
    lane = iota((NEAR, 128), 1)
    digits = jnp.where(lane == M, local_row // 64 + 1, jnp.where(lane == M + 1, local_row % 64 + 1, 0))
    tokens = wide_ref[...] + digits.astype(F32)
    near_codes_ref[...] = tokens.T[0:M].astype(I32) - 1

    level32, level128 = levels(32, NEAR), levels(128, NEAR)

    def count(side, carry):
        acc = jnp.zeros((32, 128), F32)
        for j in range(16):
            row = near_codes_ref[pl.ds(side * 16 + j, 1), :]
            upper = onehot((row >> 3).astype(F32).astype(BF), level32)
            lower = onehot(((row & 7) + 8 * j).astype(F32).astype(BF), level128)
            acc = acc + lax.dot_general(upper, lower, NT, preferred_element_type=F32)
        counts_ref[pl.ds(pl.multiple_of(side * 32, 32), 32), :] = acc
        return carry

    lax.fori_loop(0, 4, count, 0)
    column = iota((1, 128), 1)
    count_position = ((column % 32) * 4 + column // 32) * SLOT + CAP
    place_of = jnp.concatenate([position, count_position], axis=1)
    payload = jnp.concatenate([tokens.astype(BF), counts_ref[...].astype(BF)], axis=0)

    def build(i, carry):
        place = jnp.where(iota((256, NEAR + 128), 0) + i * 256 == place_of, 1.0, 0.0).astype(BF)
        rows = jnp.dot(place, payload, preferred_element_type=F32)
        message_ref[pl.ds(i * 16, 16)] = rows.astype(BF).reshape(16, SLOT, 128)
        return carry

    lax.fori_loop(0, DEVICES * SLOT // 256, build, 0)
    pl.semaphore_wait(barrier, DEVICES - 1)

    def post(step, carry):
        other = (me + step) % DEVICES
        remote(
            message_ref.at[other], arrived_ref.at[me], message_send, message_recv, (other // 4, other % 4)
        ).start()
        return carry

    lax.fori_loop(1, DEVICES, post, 0)
    arrived_ref[me] = message_ref[me]

    for i in range(8):
        rows = pl.ds(i * 128, 128)
        table_book_ref[rows, :] = book_ref[rows, :].astype(F32)

    def decode(codes, target, width):
        def step(i, carry):
            for j in range(8):
                m = i * 8 + j
                row = codes[pl.ds(m, 1), :]
                for block in range(width // 128):
                    span = slice(block * 128, (block + 1) * 128)
                    index = jnp.broadcast_to(row[:, span], (8, 128))
                    low, high = index & 127, index >= 128
                    halves = []
                    for half in range(2):
                        start = pl.multiple_of(m * DS + 8 * half, 8)
                        first = jnp.take_along_axis(table_book_ref[pl.ds(start, 8), 0:128], low, axis=1)
                        second = jnp.take_along_axis(table_book_ref[pl.ds(start, 8), 128:256], low, axis=1)
                        halves.append(jnp.where(high, second, first))
                    target[pl.ds(pl.multiple_of(m * DS, DS), DS), span] = jnp.concatenate(halves, 0).astype(BF)
            return carry

        lax.fori_loop(0, M // 8, step, 0)

    def rotate(source, width):
        def step(i, carry):
            columns = pl.ds(pl.multiple_of(i * 256, 256), 256)
            turned = lax.dot_general(rotation_ref[:, columns], source[...], TT, preferred_element_type=F32)
            upper = turned.astype(BF)
            lower = (turned - upper.astype(F32)).astype(BF)
            turned_ref[pl.ds(i * 16, 16), 0:DS, 0:width] = upper.reshape(16, DS, width)
            turned_ref[pl.ds(i * 16, 16), DS : 2 * DS, 0:width] = lower.reshape(16, DS, width)
            return carry

        lax.fori_loop(0, 4, step, 0)

    def group(codes, g, width):
        level = levels(128, width)
        upper, lower = [], []
        for j in range(8):
            row = codes[pl.ds(g * 8 + j, 1), :]
            picked = onehot((row & 127).astype(F32).astype(BF), level)
            high = jnp.broadcast_to((row >> 7).astype(F32).astype(BF), (2 * DS, width))
            values = turned_ref[g * 8 + j, :, 0:width]
            zero = jnp.zeros_like(values)
            masked = jnp.concatenate(
                [jnp.where(high == jnp.asarray(0, BF), values, zero), jnp.where(high == jnp.asarray(1, BF), values, zero)],
                0,
            )
            both = lax.dot_general(masked, picked, NT, preferred_element_type=F32)
            lower.append(both[0:16] + both[16:32])
            upper.append(both[32:48] + both[48:64])
        return jnp.concatenate(lower, 0).T, jnp.concatenate(upper, 0).T

    loads[0].wait()
    loads[1].wait()
    decode(near_codes_ref, near_reb_ref, NEAR)

    def near_cross(i, carry):
        columns = pl.ds(pl.multiple_of(i * 256, 256), 256)
        block = lax.dot_general(vectors_ref[:, columns], near_reb_ref[...], TT, preferred_element_type=F32)
        cross_ref[i] = block.reshape(4, 2, 4, 8, D)
        return carry

    lax.fori_loop(0, 4, near_cross, 0)
    rotate(vectors_ref, NEAR)

    def near_total(g, carry):
        lower, upper = group(near_codes_ref, g, NEAR)
        total_ref[g % 2, 0:2, :, :, g // 2] = lower.reshape(2, 4, 2, 8, 128)
        total_ref[g % 2, 2:4, :, :, g // 2] = upper.reshape(2, 4, 2, 8, 128)
        return carry

    lax.fori_loop(0, 8, near_total, 0)

    def widen(i, carry):
        chunk_load(i).wait()

        def part(k, inner):
            source = chunk_ref.at[i % 2]
            for c in range(8):
                piece = source[pl.ds(pl.multiple_of(k * 16, 16), 16), c * 128 : (c + 1) * 128].astype(F32)
                start = pl.multiple_of((i * (CHUNK // 16) + k) * 128 + c * 8, 8)
                table_ref[pl.ds(start, 8), :] = piece[0:8]
                table_ref[pl.ds(pl.multiple_of(start + 64, 8), 8), :] = piece[8:16]
            return inner

        lax.fori_loop(0, CHUNK // 16, part, 0)

        @pl.when(i + 2 < LISTS // CHUNK)
        def _():
            chunk_load(i + 2).start()

        return carry

    lax.fori_loop(0, LISTS // CHUNK, widen, 0)
    table_ref[LISTS * 8 : LISTS * 8 + 64, :] = jnp.zeros((64, 128), F32)

    drain(arrived_ref.at[pl.ds(0, DEVICES - 1)], message_recv)
    for i in range(8):
        arrived_wide_ref[i * 256 : (i + 1) * 256] = arrived_ref[i * 16 : (i + 1) * 16].astype(F32).reshape(256, 128)
    for j in range(CAP):
        turned_over = arrived_wide_ref[pl.ds(j, DEVICES, stride=SLOT), :].T.astype(I32) - 1
        far_codes_ref[:, j * 128 : (j + 1) * 128] = turned_over[0:M]
        upper, lower = turned_over[M : M + 1], turned_over[M + 1 : M + 2]
        row_ref[j : j + 1, :] = jnp.clip(jnp.where(upper < 0, LISTS, upper * 64 + lower), 0, LISTS)
    for j in range(CAP, 16):
        row_ref[j : j + 1, :] = jnp.zeros((1, 128), I32)
    counted = jnp.sum(arrived_wide_ref[pl.ds(CAP, DEVICES, stride=SLOT), :], axis=0, keepdims=True)
    fetch = pltpu.make_async_copy(row_ref, row_smem, local_sem.at[2])
    fetch.start()
    decode(far_codes_ref, far_reb_ref, FAR)
    fetch.wait()

    def gather(j, carry):
        def take(k, inner):
            for s in range(8):
                row = row_smem[j, k * 8 + s]
                piece = table_ref[pl.ds((row // 8) * 64 + row % 8, 8, stride=8), :]
                stage_ref[pl.ds(k * 64 + s, 8, stride=8), :] = piece
            return inner

        lax.fori_loop(0, 16, take, 0)
        block = stage_ref[...].reshape(16, 8, 8, 128)
        for c in range(8):
            far_x_ref[pl.ds(pl.multiple_of(j * 128, 128), 128), c * 128 : (c + 1) * 128] = (
                -block[:, c].reshape(128, 128)
            ).astype(BF)
        return carry

    lax.fori_loop(0, CAP, gather, 0)

    def cross_core(i):
        return remote(
            cross_ref.at[i, :, 1 - core],
            cross_half_ref.at[i],
            cross_core_send.at[i],
            cross_core_recv.at[i],
            mate,
        )

    def far_cross(i, carry):
        columns = pl.ds(pl.multiple_of(i * 256, 256), 256)
        block = lax.dot_general(far_x_ref[:, columns], far_reb_ref[...], TT, preferred_element_type=F32)
        cross_ref[i] += block.reshape(4, 2, 4, 8, D)
        cross_core(i).start()
        return carry

    lax.fori_loop(0, 4, far_cross, 0)
    rotate(far_x_ref, FAR)

    def join(i, carry):
        cross_core(i).wait_recv()
        cross_half_ref[i] += cross_ref[i, :, core]
        return carry

    lax.fori_loop(0, 4, join, 0)

    def slab(p, value, half):
        begin, end, axis, _ = PARTS[p]
        rest = [d for d in DIMS if d != axis]
        index = []
        for d in DIMS:
            if d == axis:
                index.append(value)
            elif d == rest[0]:
                index.append(pl.ds(half * 2, 2))
            else:
                index.append(slice(None))
        return cross_half_ref.at[tuple(index) + (slice(None), slice(begin, end))]

    def ring(p, slot, value, half, way):
        axis = PARTS[p][2]
        return remote(
            slab(p, value, half),
            ring_refs[p].at[slot],
            ring_send.at[p, slot],
            ring_recv.at[p, slot],
            device(**{axis: (at[axis] + way) % 4}),
        )

    def around(p):
        here = at[PARTS[p][2]]
        return here, (here + 1) % 4, (here + 2) % 4, (here + 3) % 4

    first, second = [], []
    for p in range(3):
        here, after, beyond, before = around(p)
        copies = [
            ring(p, 0, beyond, 0, 1),
            ring(p, 1, beyond, 1, 3),
            ring(p, 2, after, 1, 1),
            ring(p, 3, before, 0, 3),
        ]
        for copy in copies:
            copy.start()
        first.append(copies)

    def side(q):
        return (y + 1 + q) % 4

    def total_core(q):
        return remote(
            total_ref.at[:, :, :, 1 - core, side(q)],
            total_half_ref.at[q],
            total_core_send.at[q],
            total_core_recv.at[q],
            mate,
        )

    def total_side(q):
        return remote(
            total_half_ref.at[q],
            total_side_ref.at[q],
            total_side_send.at[q],
            total_side_recv.at[q],
            (r, side(q)),
        )

    def far_total(q):
        def step(half, carry):
            lower, upper = group(far_codes_ref, side(q) * 2 + half, FAR)
            total_ref[half, 0:2, :, :, side(q)] += lower.reshape(2, 4, 2, 8, 128)
            total_ref[half, 2:4, :, :, side(q)] += upper.reshape(2, 4, 2, 8, 128)
            return carry

        lax.fori_loop(0, 2, step, 0)
        total_core(q).start()

    def pass_on(q):
        total_core(q).wait_recv()
        total_half_ref[q] += total_ref[:, :, :, core, side(q)]
        if q < 3:
            total_side(q).start()

    far_total(0)
    far_total(1)
    pass_on(0)
    for p in range(3):
        here, after, beyond, before = around(p)
        first[p][0].wait_recv()
        target = slab(p, after, 0)
        target[...] += ring_refs[p][0]
        first[p][1].wait_recv()
        target = slab(p, before, 1)
        target[...] += ring_refs[p][1]
        copies = [ring(p, 4, after, 0, 1), ring(p, 5, before, 1, 3)]
        for copy in copies:
            copy.start()
        second.append(copies)
    far_total(2)
    pass_on(1)
    far_total(3)
    pass_on(2)

    def plane_lanes(p):
        return slice(PARTS[p][0], PARTS[p][1])

    def cross_plane(p, step):
        axes = PARTS[p][3]
        i, j = (at[axes[0]] + step // 4) % 4, (at[axes[1]] + step % 4) % 4
        return remote(
            cross_plane_ref.at[i, j, :, plane_lanes(p)],
            cross_got_ref.at[step, :, plane_lanes(p)],
            cross_plane_send.at[p],
            cross_plane_recv.at[p],
            device(**{axes[0]: i, axes[1]: j}),
        )

    for p in range(3):
        here = around(p)[0]
        for copy in first[p][2:] + second[p]:
            copy.wait_recv()
        got = ring_refs[p]
        cross_plane_ref[0:2, :, :, plane_lanes(p)] = slab(p, here, 0)[...] + got[3] + got[4]
        cross_plane_ref[2:4, :, :, plane_lanes(p)] = slab(p, here, 1)[...] + got[2] + got[5]

        def spread(step, carry, p=p):
            cross_plane(p, step).start()
            return carry

        lax.fori_loop(1, 16, spread, 0)

    pass_on(3)
    for q in range(3):
        total_side(q).wait_recv()
    total_plane_ref[...] = total_half_ref[3] + total_side_ref[0] + total_side_ref[1] + total_side_ref[2]

    def total_plane(step):
        i, j = (x + step // 4) % 4, (z + step % 4) % 4
        return remote(
            total_plane_ref.at[:, i, j],
            total_got_ref.at[step],
            total_plane_send,
            total_plane_recv,
            device(x=i, z=j),
        )

    def spread_total(step, carry):
        total_plane(step).start()
        return carry

    lax.fori_loop(1, 16, spread_total, 0)

    for p in range(3):
        axes = PARTS[p][3]
        drain(cross_got_ref.at[pl.ds(1, 15), :, plane_lanes(p)], cross_plane_recv.at[p])
        acc = cross_plane_ref[at[axes[0]], at[axes[1]], :, plane_lanes(p)]
        for step in range(1, 16):
            acc = acc + cross_got_ref[step, :, plane_lanes(p)]
        out_cross_ref[:, plane_lanes(p)] = acc / jnp.sqrt(jnp.float32(NEAR * DEVICES))
    drain(total_got_ref.at[pl.ds(1, 15)], total_plane_recv)
    spread_counts = jnp.broadcast_to(counted, (8, 128))
    for half in range(2):
        acc = total_plane_ref[half, x, z]
        for step in range(1, 16):
            acc = acc + total_got_ref[step, half]
        where = (half * 8 + iota((8, 128), 1) // DS) * 8 + iota((8, 128), 0)
        mean = acc / (jnp.take_along_axis(spread_counts, where, axis=1) + 1.0)
        for j in range(8):
            out_book_ref[half * 8 + j] = mean[:, j * DS : (j + 1) * DS]

    drain(message_ref.at[pl.ds(0, DEVICES - 1)], message_send)

    def left(i, carry):
        cross_core(i).wait_send()
        return carry

    lax.fori_loop(0, 4, left, 0)
    for p in range(3):
        for copy in first[p] + second[p]:
            copy.wait_send()
        drain(cross_got_ref.at[pl.ds(1, 15), :, plane_lanes(p)], cross_plane_send.at[p])
    for q in range(4):
        total_core(q).wait_send()
        if q < 3:
            total_side(q).wait_send()
    drain(total_got_ref.at[pl.ds(1, 15)], total_plane_send)


def per_device(vectors, coarse_list, list_slot, codes, centroids, rotation, codebook):
    slot_of = list_slot[coarse_list].reshape(1, NEAR)
    book = codebook.transpose(0, 2, 1).reshape(D, K)
    here = pl.BlockSpec(memory_space=VMEM)
    away = pl.BlockSpec(memory_space=ANY)
    return pl.pallas_call(
        kernel,
        out_shape=(jax.ShapeDtypeStruct((16, 8, DS), F32), jax.ShapeDtypeStruct((8, D), F32)),
        in_specs=[here, here, here, away, away, away],
        out_specs=(here, here),
        scratch_shapes=[
            VMEM((NEAR, D), BF),
            VMEM((D, D), BF),
            VMEM((2, CHUNK, D), BF),
            VMEM((LISTS * 8 + 64, 128), F32),
            VMEM((NEAR, 128), F32),
            VMEM((D, K), F32),
            VMEM((DEVICES, SLOT, 128), BF),
            VMEM((DEVICES, SLOT, 128), BF),
            VMEM((DEVICES * SLOT, 128), F32),
            VMEM((M, NEAR), I32),
            VMEM((M, FAR), I32),
            VMEM((16, 128), I32),
            pltpu.SMEM((16, 128), I32),
            VMEM((128, 128), F32),
            VMEM((D, NEAR), BF),
            VMEM((D, FAR), BF),
            VMEM((1024, 128), F32),
            VMEM((FAR, D), BF),
            VMEM((M, 2 * DS, FAR), BF),
            VMEM((4, 4, 2, 4, 8, D), F32),
            VMEM((2, 4, 4, 2, 4, 8, 128), F32),
            VMEM((4, 4, 4, 8, D), F32),
            [VMEM((6, 2, 4, 8, end - begin), F32) for begin, end, _, _ in PARTS],
            VMEM((4, 4, 8, D), F32),
            VMEM((16, 8, D), F32),
            VMEM((4, 2, 4, 4, 8, 128), F32),
            VMEM((3, 2, 4, 4, 8, 128), F32),
            VMEM((2, 4, 4, 8, 128), F32),
            VMEM((16, 2, 8, 128), F32),
            DMA((3,)),
            DMA((2,)),
            DMA,
            DMA,
            DMA((4,)),
            DMA((4,)),
            DMA((3, 6)),
            DMA((3, 6)),
            DMA((3,)),
            DMA((3,)),
            DMA((4,)),
            DMA((4,)),
            DMA((3,)),
            DMA((3,)),
            DMA,
            DMA,
        ],
        compiler_params=pltpu.CompilerParams(
            collective_id=0, has_side_effects=True, vmem_limit_bytes=56 * 2**20
        ),
        name="refine",
    )(slot_of, codes, book, vectors, rotation, centroids)


def solution(mesh):
    placed = (
        P(("rows", "sub"), None),
        P(("rows", "sub")),
        P(),
        P(("rows", "sub"), None),
        P(("rows", "sub"), None),
        P(),
        P(),
    )
    return jax.shard_map(
        per_device,
        mesh=mesh,
        in_specs=placed,
        out_specs=(P("sub", "rows", None), P(("rows", "sub"), None)),
        check_vma=False,
    )
```

```python
import jax
import jax.numpy as jnp
from jax import lax
from jax.experimental import pallas as pl
from jax.experimental.pallas import tpu as pltpu
from jax.sharding import PartitionSpec as P

D = 1024
M = 64
K = 256
DS = 16
NEAR = 256
LISTS = 4096
DEVICES = 128
CAP = 10
SLOT = 16
FAR = CAP * DEVICES
CHUNK = 512
F32 = jnp.float32
BF = jnp.bfloat16
I32 = jnp.int32
MESH = pl.DeviceIdType.MESH
VMEM = pltpu.VMEM
ANY = pl.ANY
DMA = pltpu.SemaphoreType.DMA

PARTS = ((0, 384, "x", "zy"), (384, 768, "y", "xz"), (768, 1024, "z", "xy"))
DIMS = "xzy"
NT = (((1,), (1,)), ((), ()))
TT = (((0,), (1,)), ((), ()))


def onehot(row, level):
    return jnp.where(row == level, jnp.asarray(1, BF), jnp.asarray(0, BF))


def iota(shape, dim):
    return lax.broadcasted_iota(I32, shape, dim)


def levels(count, width):
    return iota((count, width), 0).astype(F32).astype(BF)


def drain(ref, semaphore):
    pltpu.make_async_copy(ref, ref, semaphore).wait()


def kernel(
    coarse_smem,
    coarse_ref,
    near_codes_ref,
    book_ref,
    slots_hbm,
    vectors_hbm,
    rotation_hbm,
    centroids_hbm,
    out_total_ref,
    out_counts_ref,
    out_cross_ref,
    slots_ref,
    picked_ref,
    vectors_ref,
    rotation_ref,
    chunk_ref,
    table_ref,
    table_book_ref,
    message_ref,
    arrived_ref,
    arrived_wide_ref,
    far_codes_ref,
    row_ref,
    row_smem,
    counts_ref,
    near_reb_ref,
    far_reb_ref,
    stage_ref,
    far_x_ref,
    turned_ref,
    cross_ref,
    total_ref,
    cross_half_ref,
    ring_refs,
    cross_plane_ref,
    cross_got_ref,
    total_half_ref,
    total_side_ref,
    total_plane_ref,
    total_got_ref,
    local_sem,
    chunk_sem,
    message_send,
    message_recv,
    cross_core_send,
    cross_core_recv,
    ring_send,
    ring_recv,
    cross_plane_send,
    cross_plane_recv,
    total_core_send,
    total_core_recv,
    total_side_send,
    total_side_recv,
    total_plane_send,
    total_plane_recv,
):
    r, y = lax.axis_index("rows"), lax.axis_index("sub")
    core, z, x = lax.rem(r, 2), lax.rem(lax.div(r, 2), 4), lax.div(r, 8)
    me = r * 4 + y
    at = {"x": x, "y": y, "z": z}

    def device(**place):
        spot = dict(at, **place)
        return ((spot["x"] * 4 + spot["z"]) * 2 + core, spot["y"])

    mate = (r + 1 - 2 * core, y)

    def remote(source, target, send, recv, to):
        return pltpu.make_async_remote_copy(
            src_ref=source, dst_ref=target, send_sem=send, recv_sem=recv, device_id=to, device_id_type=MESH
        )

    def others(dr, first):
        there = lax.rem(r + dr, DEVICES // 4)
        return [(there, lax.rem(y + dy, 4)) for dy in range(first, 4)]

    barrier = pltpu.get_barrier_semaphore()

    def greet(dr, first):
        for other in others(dr, first):
            pl.semaphore_signal(barrier, inc=1, device_id=other, device_id_type=MESH)

    loads = [
        pltpu.make_async_copy(vectors_hbm, vectors_ref, local_sem.at[0]),
        pltpu.make_async_copy(rotation_hbm, rotation_ref, local_sem.at[1]),
    ]
    slots_load = pltpu.make_async_copy(slots_hbm, slots_ref, local_sem.at[3])
    slots_load.start()
    greet(0, 1)

    level32, level128 = levels(32, NEAR), levels(128, NEAR)
    counts_ref[...] = jnp.zeros((128, 128), F32)

    def count(i):
        acc = jnp.zeros((32, 128), F32)
        for j in range(2):
            m = i * 2 + j
            row = near_codes_ref[pl.ds(m, 1), :]
            upper = onehot((row >> 3).astype(F32).astype(BF), level32)
            lower = onehot(((row & 7) + 8 * lax.rem(m, 16)).astype(F32).astype(BF), level128)
            acc = acc + lax.dot_general(upper, lower, NT, preferred_element_type=F32)
        counts_ref[pl.ds(pl.multiple_of(lax.div(i, 8) * 32, 32), 32), :] += acc

    def greet_and_count(dr, carry):
        greet(dr, 0)
        count(dr)
        return carry

    lax.fori_loop(1, 32, greet_and_count, 0)
    count(0)

    slots_load.wait()
    for load in loads:
        load.start()

    def chunk_load(i):
        return pltpu.make_async_copy(
            centroids_hbm.at[pl.ds(i * CHUNK, CHUNK)], chunk_ref.at[lax.rem(i, 2)], chunk_sem.at[lax.rem(i, 2)]
        )

    chunk_load(0).start()
    chunk_load(1).start()

    def look_up(i, carry):
        for s in range(16):
            line = coarse_smem[i * 16 + s] >> 7
            picked_ref[pl.ds(i * 16 + s, 1), :] = slots_ref[pl.ds(line, 1), :]
        return carry

    lax.fori_loop(0, NEAR // 16, look_up, 0)
    coarse = jnp.broadcast_to(coarse_ref[...].astype(F32), (128, NEAR)).T.astype(I32)
    mine = iota((NEAR, 128), 1) == (coarse & 127)
    slot = jnp.sum(jnp.where(mine, picked_ref[...].astype(F32), 0.0), axis=1, keepdims=True)
    down = jnp.broadcast_to(slot, (NEAR, NEAR))
    along = down.T.astype(I32)
    down = down.astype(I32)

    owner = along >> 12
    same = (owner == (down >> 12)) & (iota((NEAR, NEAR), 0) < iota((NEAR, NEAR), 1))
    rank = jnp.sum(jnp.where(same, 1, 0), axis=0, keepdims=True)
    position = owner[0:1] * SLOT + rank
    local_row = along[0:M] & (LISTS - 1)
    line = iota((M, NEAR), 0)
    digits = jnp.where(line == 0, (local_row >> 6) + 1, jnp.where(line == 1, (local_row & 63) + 1, 0))
    tokens = jnp.concatenate([near_codes_ref[...] + 1, digits], axis=0).astype(F32).T
    column = iota((1, 128), 1)
    count_position = ((column & 31) * 4 + (column >> 5)) * SLOT + CAP
    place_of = jnp.concatenate([position, count_position], axis=1)
    payload = jnp.concatenate([tokens.astype(BF), counts_ref[...].astype(BF)], axis=0)

    def build(i, carry):
        place = jnp.where(iota((256, NEAR + 128), 0) + i * 256 == place_of, 1.0, 0.0).astype(BF)
        rows = jnp.dot(place, payload, preferred_element_type=F32)
        message_ref[pl.ds(i * 16, 16)] = rows.astype(BF).reshape(16, SLOT, 128)
        return carry

    lax.fori_loop(0, DEVICES * SLOT // 256, build, 0)
    pl.semaphore_wait(barrier, DEVICES - 1)

    def post(dr, first):
        for other in others(dr, first):
            remote(
                message_ref.at[other[0] * 4 + other[1]], arrived_ref.at[me], message_send, message_recv, other
            ).start()

    post(0, 1)

    def post_row(dr, carry):
        post(dr, 0)
        return carry

    lax.fori_loop(1, DEVICES // 4, post_row, 0)
    arrived_ref[me] = message_ref[me]

    for i in range(8):
        rows = pl.ds(i * 128, 128)
        table_book_ref[rows, :] = book_ref[rows, :].astype(F32)

    def decode(codes, target, width):
        def step(i, carry):
            for j in range(8):
                m = i * 8 + j
                row = codes[pl.ds(m, 1), :]
                for block in range(width // 128):
                    span = slice(block * 128, (block + 1) * 128)
                    index = jnp.broadcast_to(row[:, span], (8, 128))
                    low, high = index & 127, index >= 128
                    halves = []
                    for half in range(2):
                        start = pl.multiple_of(m * DS + 8 * half, 8)
                        first = jnp.take_along_axis(table_book_ref[pl.ds(start, 8), 0:128], low, axis=1)
                        second = jnp.take_along_axis(table_book_ref[pl.ds(start, 8), 128:256], low, axis=1)
                        halves.append(jnp.where(high, second, first))
                    target[pl.ds(pl.multiple_of(m * DS, DS), DS), span] = jnp.concatenate(halves, 0).astype(BF)
            return carry

        lax.fori_loop(0, M // 8, step, 0)

    def rotate(source, width):
        def step(i, carry):
            columns = pl.ds(pl.multiple_of(i * 256, 256), 256)
            turned = lax.dot_general(rotation_ref[:, columns], source[...], TT, preferred_element_type=F32)
            upper = turned.astype(BF)
            lower = (turned - upper.astype(F32)).astype(BF)
            turned_ref[pl.ds(i * 16, 16), 0:DS, 0:width] = upper.reshape(16, DS, width)
            turned_ref[pl.ds(i * 16, 16), DS : 2 * DS, 0:width] = lower.reshape(16, DS, width)
            return carry

        lax.fori_loop(0, 4, step, 0)

    def group(codes, g, width):
        level = levels(128, width)
        upper, lower = [], []
        for j in range(8):
            row = codes[pl.ds(g * 8 + j, 1), :]
            picked = onehot((row & 127).astype(F32).astype(BF), level)
            high = jnp.broadcast_to((row >> 7).astype(F32).astype(BF), (2 * DS, width))
            values = turned_ref[g * 8 + j, :, 0:width]
            zero = jnp.zeros_like(values)
            masked = jnp.concatenate(
                [jnp.where(high == jnp.asarray(0, BF), values, zero), jnp.where(high == jnp.asarray(1, BF), values, zero)],
                0,
            )
            both = lax.dot_general(masked, picked, NT, preferred_element_type=F32)
            lower.append(both[0:16] + both[16:32])
            upper.append(both[32:48] + both[48:64])
        return jnp.concatenate(lower, 0).T, jnp.concatenate(upper, 0).T

    loads[0].wait()
    loads[1].wait()
    decode(near_codes_ref, near_reb_ref, NEAR)

    def near_cross(i, carry):
        columns = pl.ds(pl.multiple_of(i * 256, 256), 256)
        block = lax.dot_general(vectors_ref[:, columns], near_reb_ref[...], TT, preferred_element_type=F32)
        cross_ref[i] = block.reshape(4, 2, 4, 8, D)
        return carry

    lax.fori_loop(0, 4, near_cross, 0)
    rotate(vectors_ref, NEAR)

    def near_total(g, carry):
        lower, upper = group(near_codes_ref, g, NEAR)
        total_ref[g % 2, 0:2, :, :, g // 2] = lower.reshape(2, 4, 2, 8, 128)
        total_ref[g % 2, 2:4, :, :, g // 2] = upper.reshape(2, 4, 2, 8, 128)
        return carry

    lax.fori_loop(0, 8, near_total, 0)

    def widen(i, carry):
        chunk_load(i).wait()

        def part(k, inner):
            source = chunk_ref.at[lax.rem(i, 2)]
            for c in range(8):
                piece = source[pl.ds(pl.multiple_of(k * 16, 16), 16), c * 128 : (c + 1) * 128].astype(F32)
                start = pl.multiple_of((i * (CHUNK // 16) + k) * 128 + c * 8, 8)
                table_ref[pl.ds(start, 8), :] = piece[0:8]
                table_ref[pl.ds(pl.multiple_of(start + 64, 8), 8), :] = piece[8:16]
            return inner

        lax.fori_loop(0, CHUNK // 16, part, 0)

        @pl.when(i + 2 < LISTS // CHUNK)
        def _():
            chunk_load(i + 2).start()

        return carry

    lax.fori_loop(0, LISTS // CHUNK, widen, 0)
    table_ref[LISTS * 8 : LISTS * 8 + 64, :] = jnp.zeros((64, 128), F32)

    drain(arrived_ref.at[pl.ds(0, DEVICES - 1)], message_recv)
    for i in range(8):
        arrived_wide_ref[i * 256 : (i + 1) * 256] = arrived_ref[i * 16 : (i + 1) * 16].astype(F32).reshape(256, 128)
    for j in range(CAP):
        turned_over = arrived_wide_ref[pl.ds(j, DEVICES, stride=SLOT), :].T.astype(I32) - 1
        far_codes_ref[:, j * 128 : (j + 1) * 128] = turned_over[0:M]
        upper, lower = turned_over[M : M + 1], turned_over[M + 1 : M + 2]
        row = jnp.clip(jnp.where(upper < 0, LISTS, upper * 64 + lower), 0, LISTS)
        row_ref[j : j + 1, :] = (row >> 3) * 64 + (row & 7)
    for j in range(CAP, 16):
        row_ref[j : j + 1, :] = jnp.zeros((1, 128), I32)
    counted = jnp.sum(arrived_wide_ref[pl.ds(CAP, DEVICES, stride=SLOT), :], axis=0, keepdims=True)
    fetch = pltpu.make_async_copy(row_ref, row_smem, local_sem.at[2])
    fetch.start()
    decode(far_codes_ref, far_reb_ref, FAR)
    fetch.wait()

    def gather(j, carry):
        def take(k, inner):
            pieces = [table_ref[pl.ds(row_smem[j, k * 16 + s], 8, stride=8), :] for s in range(16)]
            for s in range(16):
                stage_ref[pl.ds(k * 128 + (s // 8) * 64 + s % 8, 8, stride=8), :] = pieces[s]
            return inner

        lax.fori_loop(0, 8, take, 0)
        block = stage_ref[...].reshape(16, 8, 8, 128)
        for c in range(8):
            far_x_ref[pl.ds(pl.multiple_of(j * 128, 128), 128), c * 128 : (c + 1) * 128] = (
                -block[:, c].reshape(128, 128)
            ).astype(BF)
        return carry

    lax.fori_loop(0, CAP, gather, 0)

    def cross_core(i):
        return remote(
            cross_ref.at[i, :, 1 - core],
            cross_half_ref.at[i],
            cross_core_send.at[i],
            cross_core_recv.at[i],
            mate,
        )

    def far_cross(i, carry):
        columns = pl.ds(pl.multiple_of(i * 256, 256), 256)
        block = lax.dot_general(far_x_ref[:, columns], far_reb_ref[...], TT, preferred_element_type=F32)
        cross_ref[i] += block.reshape(4, 2, 4, 8, D)
        cross_core(i).start()
        return carry

    lax.fori_loop(0, 4, far_cross, 0)
    rotate(far_x_ref, FAR)

    def join(i, carry):
        cross_core(i).wait_recv()
        cross_half_ref[i] += cross_ref[i, :, core]
        return carry

    lax.fori_loop(0, 4, join, 0)

    def slab(p, value, half):
        begin, end, axis, _ = PARTS[p]
        rest = [d for d in DIMS if d != axis]
        index = []
        for d in DIMS:
            if d == axis:
                index.append(value)
            elif d == rest[0]:
                index.append(pl.ds(half * 2, 2))
            else:
                index.append(slice(None))
        return cross_half_ref.at[tuple(index) + (slice(None), slice(begin, end))]

    def ring(p, slot, value, half, way):
        axis = PARTS[p][2]
        return remote(
            slab(p, value, half),
            ring_refs[p].at[slot],
            ring_send.at[p, slot],
            ring_recv.at[p, slot],
            device(**{axis: lax.rem(at[axis] + way, 4)}),
        )

    def around(p):
        here = at[PARTS[p][2]]
        return here, lax.rem(here + 1, 4), lax.rem(here + 2, 4), lax.rem(here + 3, 4)

    first, second = [], []
    for p in range(3):
        here, after, beyond, before = around(p)
        copies = [
            ring(p, 0, beyond, 0, 1),
            ring(p, 1, beyond, 1, 3),
            ring(p, 2, after, 1, 1),
            ring(p, 3, before, 0, 3),
        ]
        for copy in copies:
            copy.start()
        first.append(copies)

    def side(q):
        return lax.rem(y + 1 + q, 4)

    def total_core(q):
        return remote(
            total_ref.at[:, :, :, 1 - core, side(q)],
            total_half_ref.at[q],
            total_core_send.at[q],
            total_core_recv.at[q],
            mate,
        )

    def total_side(q):
        return remote(
            total_half_ref.at[q],
            total_side_ref.at[q],
            total_side_send.at[q],
            total_side_recv.at[q],
            (r, side(q)),
        )

    def far_total(q):
        def step(half, carry):
            lower, upper = group(far_codes_ref, side(q) * 2 + half, FAR)
            total_ref[half, 0:2, :, :, side(q)] += lower.reshape(2, 4, 2, 8, 128)
            total_ref[half, 2:4, :, :, side(q)] += upper.reshape(2, 4, 2, 8, 128)
            return carry

        lax.fori_loop(0, 2, step, 0)
        total_core(q).start()

    def pass_on(q):
        total_core(q).wait_recv()
        total_half_ref[q] += total_ref[:, :, :, core, side(q)]
        if q < 3:
            total_side(q).start()

    far_total(0)
    far_total(1)
    pass_on(0)
    for p in range(3):
        here, after, beyond, before = around(p)
        first[p][0].wait_recv()
        target = slab(p, after, 0)
        target[...] += ring_refs[p][0]
        first[p][1].wait_recv()
        target = slab(p, before, 1)
        target[...] += ring_refs[p][1]
        copies = [ring(p, 4, after, 0, 1), ring(p, 5, before, 1, 3)]
        for copy in copies:
            copy.start()
        second.append(copies)
    far_total(2)
    pass_on(1)
    far_total(3)
    pass_on(2)

    def plane_lanes(p):
        return slice(PARTS[p][0], PARTS[p][1])

    def spread(start):
        for j in range(1, 4):
            start(0, j)

        def row(i, carry):
            for j in range(4):
                start(i, j)
            return carry

        lax.fori_loop(1, 4, row, 0)

    def cross_plane(p, di, dj):
        axes = PARTS[p][3]
        i, j = lax.rem(at[axes[0]] + di, 4), lax.rem(at[axes[1]] + dj, 4)
        remote(
            cross_plane_ref.at[i, j, :, plane_lanes(p)],
            cross_got_ref.at[di * 4 + dj, :, plane_lanes(p)],
            cross_plane_send.at[p],
            cross_plane_recv.at[p],
            device(**{axes[0]: i, axes[1]: j}),
        ).start()

    for p in range(3):
        here = around(p)[0]
        for copy in first[p][2:] + second[p]:
            copy.wait_recv()
        got = ring_refs[p]
        cross_plane_ref[0:2, :, :, plane_lanes(p)] = slab(p, here, 0)[...] + got[3] + got[4]
        cross_plane_ref[2:4, :, :, plane_lanes(p)] = slab(p, here, 1)[...] + got[2] + got[5]
        spread(lambda di, dj, p=p: cross_plane(p, di, dj))

    pass_on(3)
    for q in range(3):
        total_side(q).wait_recv()
    total_plane_ref[...] = total_half_ref[3] + total_side_ref[0] + total_side_ref[1] + total_side_ref[2]

    def total_plane(di, dj):
        i, j = lax.rem(x + di, 4), lax.rem(z + dj, 4)
        remote(
            total_plane_ref.at[:, i, j],
            total_got_ref.at[di * 4 + dj],
            total_plane_send,
            total_plane_recv,
            device(x=i, z=j),
        ).start()

    spread(total_plane)
    for p in range(3):
        axes = PARTS[p][3]
        drain(cross_got_ref.at[pl.ds(1, 15), :, plane_lanes(p)], cross_plane_recv.at[p])
        acc = cross_plane_ref[at[axes[0]], at[axes[1]], :, plane_lanes(p)]
        for step in range(1, 16):
            acc = acc + cross_got_ref[step, :, plane_lanes(p)]
        out_cross_ref[:, plane_lanes(p)] = acc
    drain(total_got_ref.at[pl.ds(1, 15)], total_plane_recv)
    for half in range(2):
        acc = total_plane_ref[half, x, z]
        for step in range(1, 16):
            acc = acc + total_got_ref[step, half]
        out_total_ref[half] = acc
    out_counts_ref[...] = jnp.broadcast_to(counted, (8, 128))

    drain(message_ref.at[pl.ds(0, DEVICES - 1)], message_send)

    def left(i, carry):
        cross_core(i).wait_send()
        return carry

    lax.fori_loop(0, 4, left, 0)
    for p in range(3):
        for copy in first[p] + second[p]:
            copy.wait_send()
        drain(cross_got_ref.at[pl.ds(1, 15), :, plane_lanes(p)], cross_plane_send.at[p])
    for q in range(4):
        total_core(q).wait_send()
        if q < 3:
            total_side(q).wait_send()
    drain(total_got_ref.at[pl.ds(1, 15)], total_plane_send)


def finish_kernel(total_ref, counts_ref, cross_ref, out_book_ref, out_cross_ref):
    out_cross_ref[...] = cross_ref[...] / jnp.sqrt(jnp.float32(NEAR * DEVICES))
    for half in range(2):
        where = (half * 8 + (iota((8, 128), 1) >> 4)) * 8 + iota((8, 128), 0)
        counts = jnp.take_along_axis(counts_ref[...], where, axis=1)
        mean = total_ref[half] / (counts + 1.0)
        for j in range(8):
            out_book_ref[half * 8 + j] = mean[:, j * DS : (j + 1) * DS]


def per_device(vectors, coarse_list, list_slot, codes, centroids, rotation, codebook):
    book = codebook.transpose(0, 2, 1).reshape(D, K)
    here = pl.BlockSpec(memory_space=VMEM)
    away = pl.BlockSpec(memory_space=ANY)
    total, counts, cross = pl.pallas_call(
        kernel,
        out_shape=(
            jax.ShapeDtypeStruct((2, 8, 128), F32),
            jax.ShapeDtypeStruct((8, 128), F32),
            jax.ShapeDtypeStruct((8, D), F32),
        ),
        in_specs=[pl.BlockSpec(memory_space=pltpu.SMEM), here, here, here, away, away, away, away],
        out_specs=(here, here, here),
        scratch_shapes=[
            VMEM((LISTS, 128), I32),
            VMEM((NEAR, 128), I32),
            VMEM((NEAR, D), BF),
            VMEM((D, D), BF),
            VMEM((2, CHUNK, D), BF),
            VMEM((LISTS * 8 + 64, 128), F32),
            VMEM((D, K), F32),
            VMEM((DEVICES, SLOT, 128), BF),
            VMEM((DEVICES, SLOT, 128), BF),
            VMEM((DEVICES * SLOT, 128), F32),
            VMEM((M, FAR), I32),
            VMEM((16, 128), I32),
            pltpu.SMEM((16, 128), I32),
            VMEM((128, 128), F32),
            VMEM((D, NEAR), BF),
            VMEM((D, FAR), BF),
            VMEM((1024, 128), F32),
            VMEM((FAR, D), BF),
            VMEM((M, 2 * DS, FAR), BF),
            VMEM((4, 4, 2, 4, 8, D), F32),
            VMEM((2, 4, 4, 2, 4, 8, 128), F32),
            VMEM((4, 4, 4, 8, D), F32),
            [VMEM((6, 2, 4, 8, end - begin), F32) for begin, end, _, _ in PARTS],
            VMEM((4, 4, 8, D), F32),
            VMEM((16, 8, D), F32),
            VMEM((4, 2, 4, 4, 8, 128), F32),
            VMEM((3, 2, 4, 4, 8, 128), F32),
            VMEM((2, 4, 4, 8, 128), F32),
            VMEM((16, 2, 8, 128), F32),
            DMA((4,)),
            DMA((2,)),
            DMA,
            DMA,
            DMA((4,)),
            DMA((4,)),
            DMA((3, 6)),
            DMA((3, 6)),
            DMA((3,)),
            DMA((3,)),
            DMA((4,)),
            DMA((4,)),
            DMA((3,)),
            DMA((3,)),
            DMA,
            DMA,
        ],
        compiler_params=pltpu.CompilerParams(
            collective_id=0, has_side_effects=True, vmem_limit_bytes=56 * 2**20
        ),
        name="refine",
    )(
        coarse_list,
        coarse_list.reshape(1, NEAR),
        codes.T,
        book,
        list_slot.reshape(LISTS, 128),
        vectors,
        rotation,
        centroids,
    )
    return pl.pallas_call(
        finish_kernel,
        out_shape=(jax.ShapeDtypeStruct((16, 8, DS), F32), jax.ShapeDtypeStruct((8, D), F32)),
        in_specs=[here] * 3,
        out_specs=(here, here),
        name="finish",
    )(total, counts, cross)


def solution(mesh):
    placed = (
        P(("rows", "sub"), None),
        P(("rows", "sub")),
        P(),
        P(("rows", "sub"), None),
        P(("rows", "sub"), None),
        P(),
        P(),
    )
    return jax.shard_map(
        per_device,
        mesh=mesh,
        in_specs=placed,
        out_specs=(P("sub", "rows", None), P(("rows", "sub"), None)),
        check_vma=False,
    )
```

```python
import jax
import jax.numpy as jnp
from jax import lax
from jax.experimental import pallas as pl
from jax.experimental.pallas import tpu as pltpu
from jax.sharding import PartitionSpec as P

D = 1024
M = 64
K = 256
DS = 16
NEAR = 256
LISTS = 4096
DEVICES = 128
CAP = 10
SLOT = 16
FAR = CAP * DEVICES
CHUNK = 512
F32 = jnp.float32
BF = jnp.bfloat16
I32 = jnp.int32
MESH = pl.DeviceIdType.MESH
VMEM = pltpu.VMEM
ANY = pl.ANY
DMA = pltpu.SemaphoreType.DMA

PARTS = ((0, 384, "x", "zy"), (384, 768, "y", "xz"), (768, 1024, "z", "xy"))
NT = (((1,), (1,)), ((), ()))
TT = (((0,), (1,)), ((), ()))


def onehot(row, level):
    return jnp.where(row == level, jnp.asarray(1, BF), jnp.asarray(0, BF))


def iota(shape, dim):
    return lax.broadcasted_iota(I32, shape, dim)


def levels(count, width):
    return iota((count, width), 0).astype(F32).astype(BF)


def drain(ref, semaphore):
    pltpu.make_async_copy(ref, ref, semaphore).wait()


def kernel(
    coarse_smem,
    coarse_ref,
    near_codes_ref,
    book_ref,
    slots_hbm,
    vectors_hbm,
    rotation_hbm,
    centroids_hbm,
    out_total_ref,
    out_counts_ref,
    out_cross_ref,
    slots_ref,
    picked_ref,
    vectors_ref,
    rotation_ref,
    chunk_ref,
    table_ref,
    table_book_ref,
    message_ref,
    arrived_ref,
    arrived_wide_ref,
    far_codes_ref,
    far_blocks_ref,
    row_ref,
    row_smem,
    counts_ref,
    near_reb_ref,
    far_reb_ref,
    stage_ref,
    far_x_ref,
    turned_ref,
    cross_ref,
    total_ref,
    cross_half_ref,
    over_x_ref,
    over_y_ref,
    over_z_ref,
    cross_plane_ref,
    cross_got_ref,
    total_half_ref,
    total_side_ref,
    total_plane_ref,
    total_got_ref,
    local_sem,
    chunk_sem,
    message_send,
    message_recv,
    cross_core_send,
    cross_core_recv,
    over_x_send,
    over_x_recv,
    over_y_send,
    over_y_recv,
    over_z_send,
    over_z_recv,
    cross_plane_send,
    cross_plane_recv,
    total_core_send,
    total_core_recv,
    total_side_send,
    total_side_recv,
    total_plane_send,
    total_plane_recv,
):
    r, y = lax.axis_index("rows"), lax.axis_index("sub")
    core, z, x = lax.rem(r, 2), lax.rem(lax.div(r, 2), 4), lax.div(r, 8)
    me = r * 4 + y
    at = {"x": x, "y": y, "z": z}

    def device(**place):
        spot = dict(at, **place)
        return ((spot["x"] * 4 + spot["z"]) * 2 + core, spot["y"])

    mate = (r + 1 - 2 * core, y)

    def remote(source, target, send, recv, to):
        return pltpu.make_async_remote_copy(
            src_ref=source, dst_ref=target, send_sem=send, recv_sem=recv, device_id=to, device_id_type=MESH
        )

    def others(dr, first):
        there = lax.rem(r + dr, DEVICES // 4)
        return [(there, lax.rem(y + dy, 4)) for dy in range(first, 4)]

    barrier = pltpu.get_barrier_semaphore()

    def greet(dr, first):
        for other in others(dr, first):
            pl.semaphore_signal(barrier, inc=1, device_id=other, device_id_type=MESH)

    loads = [
        pltpu.make_async_copy(vectors_hbm, vectors_ref, local_sem.at[0]),
        pltpu.make_async_copy(rotation_hbm, rotation_ref, local_sem.at[1]),
    ]
    slots_load = pltpu.make_async_copy(slots_hbm, slots_ref, local_sem.at[3])
    slots_load.start()

    level32, level128 = levels(32, NEAR), levels(128, NEAR)
    counts_ref[...] = jnp.zeros((128, 128), F32)

    def count(i):
        acc = jnp.zeros((32, 128), F32)
        for j in range(8):
            m = i * 8 + j
            row = near_codes_ref[pl.ds(m, 1), :]
            upper = onehot((row >> 3).astype(F32).astype(BF), level32)
            lower = onehot(((row & 7) + 8 * lax.rem(m, 16)).astype(F32).astype(BF), level128)
            acc = acc + lax.dot_general(upper, lower, NT, preferred_element_type=F32)
        counts_ref[pl.ds(pl.multiple_of(lax.div(i, 2) * 32, 32), 32), :] += acc

    def greet_and_count(i, carry):
        for k in range(4):
            greet(i * 4 + k, 0)
        count(i)
        return carry

    for k in range(4):
        greet(k, 1 if k == 0 else 0)
    count(jnp.int32(0))
    lax.fori_loop(1, 8, greet_and_count, 0)
    for i in range(8):
        rows = pl.ds(i * 128, 128)
        table_book_ref[rows, :] = book_ref[rows, :].astype(F32)

    slots_load.wait()
    for load in loads:
        load.start()

    def chunk_load(i):
        return pltpu.make_async_copy(
            centroids_hbm.at[pl.ds(i * CHUNK, CHUNK)], chunk_ref.at[lax.rem(i, 2)], chunk_sem.at[lax.rem(i, 2)]
        )

    chunk_load(0).start()
    chunk_load(1).start()

    def look_up(i, carry):
        for s in range(16):
            line = coarse_smem[i * 16 + s] >> 7
            picked_ref[pl.ds(i * 16 + s, 1), :] = slots_ref[pl.ds(line, 1), :]
        return carry

    lax.fori_loop(0, NEAR // 16, look_up, 0)
    coarse = jnp.broadcast_to(coarse_ref[...].astype(F32), (128, NEAR)).T.astype(I32)
    mine = iota((NEAR, 128), 1) == (coarse & 127)
    slot = jnp.sum(jnp.where(mine, picked_ref[...].astype(F32), 0.0), axis=1, keepdims=True)
    down = jnp.broadcast_to(slot, (NEAR, NEAR))
    along = down.T.astype(I32)
    down = down.astype(I32)

    owner = along >> 12
    same = (owner == (down >> 12)) & (iota((NEAR, NEAR), 0) < iota((NEAR, NEAR), 1))
    rank = jnp.sum(jnp.where(same, 1, 0), axis=0, keepdims=True)
    position = owner[0:1] * SLOT + rank
    local_row = along[0:M] & (LISTS - 1)
    line = iota((M, NEAR), 0)
    digits = jnp.where(line == 0, (local_row >> 6) + 1, jnp.where(line == 1, (local_row & 63) + 1, 0))
    tokens = jnp.concatenate([near_codes_ref[...] + 1, digits], axis=0).astype(F32).T
    column = iota((1, 128), 1)
    count_position = ((column & 31) * 4 + (column >> 5)) * SLOT + CAP
    place_of = jnp.concatenate([position, count_position], axis=1)
    payload = jnp.concatenate([tokens.astype(BF), counts_ref[...].astype(BF)], axis=0)

    def build(i, carry):
        place = jnp.where(iota((256, NEAR + 128), 0) + i * 256 == place_of, 1.0, 0.0).astype(BF)
        rows = jnp.dot(place, payload, preferred_element_type=F32)
        message_ref[pl.ds(i * 16, 16)] = rows.astype(BF).reshape(16, SLOT, 128)
        return carry

    lax.fori_loop(0, DEVICES * SLOT // 256, build, 0)
    pl.semaphore_wait(barrier, DEVICES - 1)

    def post(dr, first):
        for other in others(dr, first):
            remote(
                message_ref.at[other[0] * 4 + other[1]], arrived_ref.at[me], message_send, message_recv, other
            ).start()

    def decode(codes, target, i, span):
        for j in range(8):
            m = i * 8 + j
            index = jnp.broadcast_to(codes(m), (8, 128))
            low, high = index & 127, index >= 128
            halves = []
            for half in range(2):
                start = pl.multiple_of(m * DS + 8 * half, 8)
                first = jnp.take_along_axis(table_book_ref[pl.ds(start, 8), 0:128], low, axis=1)
                second = jnp.take_along_axis(table_book_ref[pl.ds(start, 8), 128:256], low, axis=1)
                halves.append(jnp.where(high, second, first))
            target[pl.ds(pl.multiple_of(m * DS, DS), DS), span] = jnp.concatenate(halves, 0).astype(BF)

    def near_decode(i):
        for block in range(NEAR // 128):
            span = slice(block * 128, (block + 1) * 128)
            decode(lambda m, span=span: near_codes_ref[pl.ds(m, 1), :][:, span], near_reb_ref, i, span)

    def post_and_decode(i, carry):
        for k in range(4):
            post(i * 4 + k, 0)
        near_decode(i)
        return carry

    for k in range(4):
        post(k, 1 if k == 0 else 0)
    lax.fori_loop(1, 8, post_and_decode, 0)
    near_decode(jnp.int32(0))
    arrived_ref[me] = message_ref[me]

    def rotate(source, width, begin, end):
        def step(i, carry):
            columns = pl.ds(pl.multiple_of(i * 256, 256), 256)
            turned = lax.dot_general(rotation_ref[:, columns], source[...], TT, preferred_element_type=F32)
            upper = turned.astype(BF)
            lower = (turned - upper.astype(F32)).astype(BF)
            turned_ref[pl.ds(i * 16, 16), 0:DS, 0:width] = upper.reshape(16, DS, width)
            turned_ref[pl.ds(i * 16, 16), DS : 2 * DS, 0:width] = lower.reshape(16, DS, width)
            return carry

        lax.fori_loop(begin, end, step, 0)

    def group(codes, g, width):
        level = levels(128, width)
        upper, lower = [], []
        for j in range(8):
            row = codes[pl.ds(g * 8 + j, 1), :]
            picked = onehot((row & 127).astype(F32).astype(BF), level)
            high = jnp.broadcast_to((row >> 7).astype(F32).astype(BF), (2 * DS, width))
            values = turned_ref[g * 8 + j, :, 0:width]
            zero = jnp.zeros_like(values)
            masked = jnp.concatenate(
                [jnp.where(high == jnp.asarray(0, BF), values, zero), jnp.where(high == jnp.asarray(1, BF), values, zero)],
                0,
            )
            both = lax.dot_general(masked, picked, NT, preferred_element_type=F32)
            lower.append(both[0:16] + both[16:32])
            upper.append(both[32:48] + both[48:64])
        return jnp.concatenate(lower, 0).T, jnp.concatenate(upper, 0).T

    loads[0].wait()
    loads[1].wait()

    def near_cross(i, carry):
        columns = pl.ds(pl.multiple_of(i * 256, 256), 256)
        block = lax.dot_general(vectors_ref[:, columns], near_reb_ref[...], TT, preferred_element_type=F32)
        cross_ref[i] = block.reshape(4, 2, 4, 8, D)
        return carry

    lax.fori_loop(0, 4, near_cross, 0)
    rotate(vectors_ref, NEAR, 0, 4)

    def near_total(g, carry):
        lower, upper = group(near_codes_ref, g, NEAR)
        total_ref[g % 2, 0:2, :, :, g // 2] = lower.reshape(2, 4, 2, 8, 128)
        total_ref[g % 2, 2:4, :, :, g // 2] = upper.reshape(2, 4, 2, 8, 128)
        return carry

    lax.fori_loop(0, 8, near_total, 0)

    def widen(i, carry):
        chunk_load(i).wait()

        def part(k, inner):
            source = chunk_ref.at[lax.rem(i, 2)]
            for c in range(8):
                piece = source[pl.ds(pl.multiple_of(k * 16, 16), 16), c * 128 : (c + 1) * 128].astype(F32)
                start = pl.multiple_of((i * (CHUNK // 16) + k) * 128 + c * 8, 8)
                table_ref[pl.ds(start, 8), :] = piece[0:8]
                table_ref[pl.ds(pl.multiple_of(start + 64, 8), 8), :] = piece[8:16]
            return inner

        lax.fori_loop(0, CHUNK // 16, part, 0)

        @pl.when(i + 2 < LISTS // CHUNK)
        def _():
            chunk_load(i + 2).start()

        return carry

    lax.fori_loop(0, LISTS // CHUNK, widen, 0)
    table_ref[LISTS * 8 : LISTS * 8 + 64, :] = jnp.zeros((64, 128), F32)

    drain(arrived_ref.at[pl.ds(0, DEVICES - 1)], message_recv)
    for i in range(8):
        arrived_wide_ref[i * 256 : (i + 1) * 256] = arrived_ref[i * 16 : (i + 1) * 16].astype(F32).reshape(256, 128)
    for j in range(CAP):
        turned_over = arrived_wide_ref[pl.ds(j, DEVICES, stride=SLOT), :].T.astype(I32) - 1
        far_codes_ref[:, j * 128 : (j + 1) * 128] = turned_over[0:M]
        far_blocks_ref[j] = turned_over[0:M]
        upper, lower = turned_over[M : M + 1], turned_over[M + 1 : M + 2]
        row = jnp.clip(jnp.where(upper < 0, LISTS, upper * 64 + lower), 0, LISTS)
        row_ref[j : j + 1, :] = (row >> 3) * 64 + (row & 7)
    for j in range(CAP, 16):
        row_ref[j : j + 1, :] = jnp.zeros((1, 128), I32)
    counted = jnp.sum(arrived_wide_ref[pl.ds(CAP, DEVICES, stride=SLOT), :], axis=0, keepdims=True)
    fetch = pltpu.make_async_copy(row_ref, row_smem, local_sem.at[2])
    fetch.start()
    fetch.wait()

    def gather(j, carry):
        def take(k, inner):
            pieces = [table_ref[pl.ds(row_smem[j, k * 16 + s], 8, stride=8), :] for s in range(16)]
            for s in range(16):
                stage_ref[pl.ds(k * 128 + (s // 8) * 64 + s % 8, 8, stride=8), :] = pieces[s]
            span = pl.ds(pl.multiple_of(j * 128, 128), 128)
            decode(lambda m: far_blocks_ref[j, pl.ds(m, 1), :], far_reb_ref, k, span)
            return inner

        lax.fori_loop(0, 8, take, 0)
        block = stage_ref[...].reshape(16, 8, 8, 128)
        for c in range(8):
            far_x_ref[pl.ds(pl.multiple_of(j * 128, 128), 128), c * 128 : (c + 1) * 128] = (
                -block[:, c].reshape(128, 128)
            ).astype(BF)
        return carry

    lax.fori_loop(0, CAP, gather, 0)

    def slab(q):
        return lax.rem(x + 1 + q, 4)

    def cross_core(q):
        return remote(
            cross_ref.at[slab(q), :, 1 - core],
            cross_half_ref.at[slab(q)],
            cross_core_send.at[q],
            cross_core_recv.at[q],
            mate,
        )

    def lanes(p):
        return slice(PARTS[p][0], PARTS[p][1])

    def over_x(q):
        i = slab(q)
        return remote(
            cross_half_ref.at[i, :, :, :, lanes(0)], over_x_ref.at[q], over_x_send.at[q], over_x_recv.at[q], device(x=i)
        )

    def over_y(q, s):
        i, j = slab(q), lax.rem(y + s, 4)
        return remote(
            cross_half_ref.at[i, :, j, :, lanes(1)],
            over_y_ref.at[s - 1, i],
            over_y_send.at[q, s - 1],
            over_y_recv.at[q, s - 1],
            device(y=j),
        )

    def over_z(q, s):
        i, j = slab(q), lax.rem(z + s, 4)
        return remote(
            cross_half_ref.at[i, j, :, :, lanes(2)],
            over_z_ref.at[s - 1, i],
            over_z_send.at[q, s - 1],
            over_z_recv.at[q, s - 1],
            device(z=j),
        )

    def join(q):
        cross_core(q).wait_recv()
        cross_half_ref[slab(q)] += cross_ref[slab(q), :, core]
        for s in range(1, 4):
            over_y(q, s).start()
            over_z(q, s).start()

    def far_cross(q, carry):
        i = slab(q)
        columns = pl.ds(pl.multiple_of(i * 256, 256), 256)
        block = lax.dot_general(far_x_ref[:, columns], far_reb_ref[...], TT, preferred_element_type=F32)
        cross_ref[i] += block.reshape(4, 2, 4, 8, D)
        cross_core(q).start()

        @pl.when(q >= 1)
        def _():
            join(q - 1)
            over_x(q - 1).start()

        return carry

    lax.fori_loop(0, 4, far_cross, 0)
    rotate(far_x_ref, FAR, 0, 2)
    join(3)
    rotate(far_x_ref, FAR, 2, 4)

    def side(q):
        return lax.rem(y + 1 + q, 4)

    def total_core(q):
        return remote(
            total_ref.at[:, :, :, 1 - core, side(q)],
            total_half_ref.at[q],
            total_core_send.at[q],
            total_core_recv.at[q],
            mate,
        )

    def total_side(q):
        return remote(
            total_half_ref.at[q],
            total_side_ref.at[q],
            total_side_send.at[q],
            total_side_recv.at[q],
            (r, side(q)),
        )

    def far_total(q):
        def step(half, carry):
            lower, upper = group(far_codes_ref, side(q) * 2 + half, FAR)
            total_ref[half, 0:2, :, :, side(q)] += lower.reshape(2, 4, 2, 8, 128)
            total_ref[half, 2:4, :, :, side(q)] += upper.reshape(2, 4, 2, 8, 128)
            return carry

        lax.fori_loop(0, 2, step, 0)
        total_core(q).start()

    def pass_on(q):
        total_core(q).wait_recv()
        total_half_ref[q] += total_ref[:, :, :, core, side(q)]
        if q < 3:
            total_side(q).start()

    def spread(start):
        for j in range(1, 4):
            start(0, j)

        def row(i, carry):
            for j in range(4):
                start(i, j)
            return carry

        lax.fori_loop(1, 4, row, 0)

    def cross_plane(p, di, dj):
        axes = PARTS[p][3]
        i, j = lax.rem(at[axes[0]] + di, 4), lax.rem(at[axes[1]] + dj, 4)
        remote(
            cross_plane_ref.at[i, j, :, lanes(p)],
            cross_got_ref.at[di * 4 + dj, :, lanes(p)],
            cross_plane_send.at[p],
            cross_plane_recv.at[p],
            device(**{axes[0]: i, axes[1]: j}),
        ).start()

    far_total(0)
    far_total(1)
    pass_on(0)
    far_total(2)
    pass_on(1)

    for q in range(3):
        over_x(q).wait_recv()
    cross_plane_ref[:, :, :, lanes(0)] = (
        cross_half_ref[x, :, :, :, lanes(0)] + over_x_ref[0] + over_x_ref[1] + over_x_ref[2]
    )
    spread(lambda di, dj: cross_plane(0, di, dj))

    def arrived_over(q, carry):
        for s in range(1, 4):
            over_y(q, s).wait_recv()
            over_z(q, s).wait_recv()
        return carry

    lax.fori_loop(0, 4, arrived_over, 0)
    cross_plane_ref[:, :, :, lanes(1)] = (
        cross_half_ref[:, :, y, :, lanes(1)] + over_y_ref[0] + over_y_ref[1] + over_y_ref[2]
    )
    spread(lambda di, dj: cross_plane(1, di, dj))
    cross_plane_ref[:, :, :, lanes(2)] = (
        cross_half_ref[:, z, :, :, lanes(2)] + over_z_ref[0] + over_z_ref[1] + over_z_ref[2]
    )
    spread(lambda di, dj: cross_plane(2, di, dj))
    far_total(3)
    pass_on(2)
    pass_on(3)
    for q in range(3):
        total_side(q).wait_recv()
    total_plane_ref[...] = total_half_ref[3] + total_side_ref[0] + total_side_ref[1] + total_side_ref[2]

    def total_plane(di, dj):
        i, j = lax.rem(x + di, 4), lax.rem(z + dj, 4)
        remote(
            total_plane_ref.at[:, i, j],
            total_got_ref.at[di * 4 + dj],
            total_plane_send,
            total_plane_recv,
            device(x=i, z=j),
        ).start()

    spread(total_plane)
    for p in range(3):
        axes = PARTS[p][3]
        drain(cross_got_ref.at[pl.ds(1, 15), :, lanes(p)], cross_plane_recv.at[p])
        acc = cross_plane_ref[at[axes[0]], at[axes[1]], :, lanes(p)]
        for step in range(1, 16):
            acc = acc + cross_got_ref[step, :, lanes(p)]
        out_cross_ref[:, lanes(p)] = acc
    drain(total_got_ref.at[pl.ds(1, 15)], total_plane_recv)
    for half in range(2):
        acc = total_plane_ref[half, x, z]
        for step in range(1, 16):
            acc = acc + total_got_ref[step, half]
        out_total_ref[half] = acc
    out_counts_ref[...] = jnp.broadcast_to(counted, (8, 128))

    drain(message_ref.at[pl.ds(0, DEVICES - 1)], message_send)

    def left(q, carry):
        cross_core(q).wait_send()
        for s in range(1, 4):
            over_y(q, s).wait_send()
            over_z(q, s).wait_send()
        return carry

    lax.fori_loop(0, 4, left, 0)
    for p in range(3):
        over_x(p).wait_send()
        drain(cross_got_ref.at[pl.ds(1, 15), :, lanes(p)], cross_plane_send.at[p])
    for q in range(4):
        total_core(q).wait_send()
        if q < 3:
            total_side(q).wait_send()
    drain(total_got_ref.at[pl.ds(1, 15)], total_plane_send)


def finish_kernel(total_ref, counts_ref, cross_ref, out_book_ref, out_cross_ref):
    out_cross_ref[...] = cross_ref[...] / jnp.sqrt(jnp.float32(NEAR * DEVICES))
    for half in range(2):
        where = (half * 8 + (iota((8, 128), 1) >> 4)) * 8 + iota((8, 128), 0)
        counts = jnp.take_along_axis(counts_ref[...], where, axis=1)
        mean = total_ref[half] / (counts + 1.0)
        for j in range(8):
            out_book_ref[half * 8 + j] = mean[:, j * DS : (j + 1) * DS]


def per_device(vectors, coarse_list, list_slot, codes, centroids, rotation, codebook):
    book = codebook.transpose(0, 2, 1).reshape(D, K)
    here = pl.BlockSpec(memory_space=VMEM)
    away = pl.BlockSpec(memory_space=ANY)
    total, counts, cross = pl.pallas_call(
        kernel,
        out_shape=(
            jax.ShapeDtypeStruct((2, 8, 128), F32),
            jax.ShapeDtypeStruct((8, 128), F32),
            jax.ShapeDtypeStruct((8, D), F32),
        ),
        in_specs=[pl.BlockSpec(memory_space=pltpu.SMEM), here, here, here, away, away, away, away],
        out_specs=(here, here, here),
        scratch_shapes=[
            VMEM((LISTS, 128), I32),
            VMEM((NEAR, 128), I32),
            VMEM((NEAR, D), BF),
            VMEM((D, D), BF),
            VMEM((2, CHUNK, D), BF),
            VMEM((LISTS * 8 + 64, 128), F32),
            VMEM((D, K), F32),
            VMEM((DEVICES, SLOT, 128), BF),
            VMEM((DEVICES, SLOT, 128), BF),
            VMEM((DEVICES * SLOT, 128), F32),
            VMEM((M, FAR), I32),
            VMEM((CAP, M, 128), I32),
            VMEM((16, 128), I32),
            pltpu.SMEM((16, 128), I32),
            VMEM((128, 128), F32),
            VMEM((D, NEAR), BF),
            VMEM((D, FAR), BF),
            VMEM((1024, 128), F32),
            VMEM((FAR, D), BF),
            VMEM((M, 2 * DS, FAR), BF),
            VMEM((4, 4, 2, 4, 8, D), F32),
            VMEM((2, 4, 4, 2, 4, 8, 128), F32),
            VMEM((4, 4, 4, 8, D), F32),
            VMEM((3, 4, 4, 8, 384), F32),
            VMEM((3, 4, 4, 8, 384), F32),
            VMEM((3, 4, 4, 8, 256), F32),
            VMEM((4, 4, 8, D), F32),
            VMEM((16, 8, D), F32),
            VMEM((4, 2, 4, 4, 8, 128), F32),
            VMEM((3, 2, 4, 4, 8, 128), F32),
            VMEM((2, 4, 4, 8, 128), F32),
            VMEM((16, 2, 8, 128), F32),
            DMA((4,)),
            DMA((2,)),
            DMA,
            DMA,
            DMA((4,)),
            DMA((4,)),
            DMA((3,)),
            DMA((3,)),
            DMA((4, 3)),
            DMA((4, 3)),
            DMA((4, 3)),
            DMA((4, 3)),
            DMA((3,)),
            DMA((3,)),
            DMA((4,)),
            DMA((4,)),
            DMA((3,)),
            DMA((3,)),
            DMA,
            DMA,
        ],
        compiler_params=pltpu.CompilerParams(
            collective_id=0, has_side_effects=True, vmem_limit_bytes=56 * 2**20
        ),
        name="refine",
    )(
        coarse_list,
        coarse_list.reshape(1, NEAR),
        codes.T,
        book,
        list_slot.reshape(LISTS, 128),
        vectors,
        rotation,
        centroids,
    )
    return pl.pallas_call(
        finish_kernel,
        out_shape=(jax.ShapeDtypeStruct((16, 8, DS), F32), jax.ShapeDtypeStruct((8, D), F32)),
        in_specs=[here] * 3,
        out_specs=(here, here),
        name="finish",
    )(total, counts, cross)


def solution(mesh):
    placed = (
        P(("rows", "sub"), None),
        P(("rows", "sub")),
        P(),
        P(("rows", "sub"), None),
        P(("rows", "sub"), None),
        P(),
        P(),
    )
    return jax.shard_map(
        per_device,
        mesh=mesh,
        in_specs=placed,
        out_specs=(P("sub", "rows", None), P(("rows", "sub"), None)),
        check_vma=False,
    )
```

```python
import jax
import jax.numpy as jnp
from jax import lax
from jax.experimental import pallas as pl
from jax.experimental.pallas import tpu as pltpu
from jax.sharding import PartitionSpec as P

D = 1024
M = 64
K = 256
DS = 16
NEAR = 256
LISTS = 4096
DEVICES = 128
CAP = 10
SLOT = 16
FAR = CAP * DEVICES
CHUNK = 512
F32 = jnp.float32
BF = jnp.bfloat16
I32 = jnp.int32
MESH = pl.DeviceIdType.MESH
VMEM = pltpu.VMEM
ANY = pl.ANY
DMA = pltpu.SemaphoreType.DMA

PARTS = ((0, 384, "x", "zy"), (384, 640, "y", "xz"), (640, 1024, "z", "xy"))
NT = (((1,), (1,)), ((), ()))
TT = (((0,), (1,)), ((), ()))


def onehot(row, level):
    return jnp.where(row == level, jnp.asarray(1, BF), jnp.asarray(0, BF))


def iota(shape, dim):
    return lax.broadcasted_iota(I32, shape, dim)


def levels(count, width):
    return iota((count, width), 0).astype(F32).astype(BF)


def drain(ref, semaphore):
    pltpu.make_async_copy(ref, ref, semaphore).wait()


def kernel(
    coarse_smem,
    coarse_ref,
    near_codes_ref,
    book_ref,
    slots_hbm,
    vectors_hbm,
    rotation_hbm,
    centroids_hbm,
    out_total_ref,
    out_counts_ref,
    out_cross_ref,
    slots_ref,
    picked_ref,
    vectors_ref,
    rotation_ref,
    chunk_ref,
    table_ref,
    table_book_ref,
    message_ref,
    arrived_ref,
    arrived_wide_ref,
    far_codes_ref,
    row_ref,
    row_smem,
    counts_ref,
    near_reb_ref,
    far_reb_ref,
    stage_ref,
    far_x_ref,
    turned_ref,
    cross_ref,
    total_ref,
    cross_half_ref,
    over_x_ref,
    over_y_ref,
    over_z_ref,
    cross_plane_ref,
    cross_got_ref,
    total_half_ref,
    total_side_ref,
    total_plane_ref,
    total_got_ref,
    local_sem,
    chunk_sem,
    message_send,
    message_recv,
    cross_core_send,
    cross_core_recv,
    over_x_send,
    over_x_recv,
    over_y_send,
    over_y_recv,
    over_z_send,
    over_z_recv,
    cross_plane_send,
    cross_plane_recv,
    total_core_send,
    total_core_recv,
    total_side_send,
    total_side_recv,
    total_plane_send,
    total_plane_recv,
):
    r, y = lax.axis_index("rows"), lax.axis_index("sub")
    core, z, x = lax.rem(r, 2), lax.rem(lax.div(r, 2), 4), lax.div(r, 8)
    me = r * 4 + y
    at = {"x": x, "y": y, "z": z}

    def device(**place):
        spot = dict(at, **place)
        return ((spot["x"] * 4 + spot["z"]) * 2 + core, spot["y"])

    mate = (r + 1 - 2 * core, y)

    def remote(source, target, send, recv, to):
        return pltpu.make_async_remote_copy(
            src_ref=source, dst_ref=target, send_sem=send, recv_sem=recv, device_id=to, device_id_type=MESH
        )

    def others(dr, first):
        there = lax.rem(r + dr, DEVICES // 4)
        return [(there, lax.rem(y + dy, 4)) for dy in range(first, 4)]

    barrier = pltpu.get_barrier_semaphore()

    def greet(dr, first):
        for other in others(dr, first):
            pl.semaphore_signal(barrier, inc=1, device_id=other, device_id_type=MESH)

    loads = [
        pltpu.make_async_copy(vectors_hbm, vectors_ref, local_sem.at[0]),
        pltpu.make_async_copy(rotation_hbm, rotation_ref, local_sem.at[1]),
    ]
    slots_load = pltpu.make_async_copy(slots_hbm, slots_ref, local_sem.at[3])
    slots_load.start()

    level32, level128 = levels(32, NEAR), levels(128, NEAR)
    counts_ref[...] = jnp.zeros((128, 128), F32)

    def count(i):
        acc = jnp.zeros((32, 128), F32)
        for j in range(8):
            m = i * 8 + j
            row = near_codes_ref[pl.ds(m, 1), :]
            upper = onehot((row >> 3).astype(F32).astype(BF), level32)
            lower = onehot(((row & 7) + 8 * lax.rem(m, 16)).astype(F32).astype(BF), level128)
            acc = acc + lax.dot_general(upper, lower, NT, preferred_element_type=F32)
        counts_ref[pl.ds(pl.multiple_of(lax.div(i, 2) * 32, 32), 32), :] += acc

    def greet_and_count(i, carry):
        for k in range(4):
            greet(i * 4 + k, 0)
        count(i)
        return carry

    for k in range(4):
        greet(k, 1 if k == 0 else 0)
    count(jnp.int32(0))
    lax.fori_loop(1, 8, greet_and_count, 0)
    for i in range(8):
        rows = pl.ds(i * 128, 128)
        table_book_ref[rows, :] = book_ref[rows, :].astype(F32)

    slots_load.wait()
    for load in loads:
        load.start()

    def chunk_load(i):
        return pltpu.make_async_copy(
            centroids_hbm.at[pl.ds(i * CHUNK, CHUNK)], chunk_ref.at[lax.rem(i, 2)], chunk_sem.at[lax.rem(i, 2)]
        )

    chunk_load(0).start()
    chunk_load(1).start()

    def look_up(i, carry):
        for s in range(16):
            line = coarse_smem[i * 16 + s] >> 7
            picked_ref[pl.ds(i * 16 + s, 1), :] = slots_ref[pl.ds(line, 1), :]
        return carry

    lax.fori_loop(0, NEAR // 16, look_up, 0)
    coarse = jnp.broadcast_to(coarse_ref[...].astype(F32), (128, NEAR)).T.astype(I32)
    mine = iota((NEAR, 128), 1) == (coarse & 127)
    slot = jnp.sum(jnp.where(mine, picked_ref[...].astype(F32), 0.0), axis=1, keepdims=True)
    down = jnp.broadcast_to(slot, (NEAR, NEAR))
    along = down.T.astype(I32)
    down = down.astype(I32)

    owner = along >> 12
    same = (owner == (down >> 12)) & (iota((NEAR, NEAR), 0) < iota((NEAR, NEAR), 1))
    rank = jnp.sum(jnp.where(same, 1, 0), axis=0, keepdims=True)
    position = owner[0:1] * SLOT + rank
    local_row = along[0:M] & (LISTS - 1)
    line = iota((M, NEAR), 0)
    digits = jnp.where(line == 0, (local_row >> 6) + 1, jnp.where(line == 1, (local_row & 63) + 1, 0))
    tokens = jnp.concatenate([near_codes_ref[...] + 1, digits], axis=0).astype(F32).T
    column = iota((1, 128), 1)
    count_position = ((column & 31) * 4 + (column >> 5)) * SLOT + CAP
    place_of = jnp.concatenate([position, count_position], axis=1)
    payload = jnp.concatenate([tokens.astype(BF), counts_ref[...].astype(BF)], axis=0)

    def build(i, carry):
        place = jnp.where(iota((256, NEAR + 128), 0) + i * 256 == place_of, 1.0, 0.0).astype(BF)
        rows = jnp.dot(place, payload, preferred_element_type=F32)
        message_ref[pl.ds(i * 16, 16)] = rows.astype(BF).reshape(16, SLOT, 128)
        return carry

    lax.fori_loop(0, DEVICES * SLOT // 256, build, 0)
    pl.semaphore_wait(barrier, DEVICES - 1)

    def post(dr, first):
        for other in others(dr, first):
            remote(
                message_ref.at[other[0] * 4 + other[1]], arrived_ref.at[me], message_send, message_recv, other
            ).start()

    def decode(codes, target, i, span):
        for j in range(8):
            m = i * 8 + j
            index = jnp.broadcast_to(codes(m), (8, 128))
            low, high = index & 127, index >= 128
            halves = []
            for half in range(2):
                start = pl.multiple_of(m * DS + 8 * half, 8)
                first = jnp.take_along_axis(table_book_ref[pl.ds(start, 8), 0:128], low, axis=1)
                second = jnp.take_along_axis(table_book_ref[pl.ds(start, 8), 128:256], low, axis=1)
                halves.append(jnp.where(high, second, first))
            target[pl.ds(pl.multiple_of(m * DS, DS), DS), span] = jnp.concatenate(halves, 0).astype(BF)

    def near_decode(i):
        for block in range(NEAR // 128):
            span = slice(block * 128, (block + 1) * 128)
            decode(lambda m, span=span: near_codes_ref[pl.ds(m, 1), :][:, span], near_reb_ref, i, span)

    def post_and_decode(i, carry):
        for k in range(4):
            post(i * 4 + k, 0)
        near_decode(i)
        return carry

    for k in range(4):
        post(k, 1 if k == 0 else 0)
    lax.fori_loop(1, 8, post_and_decode, 0)
    near_decode(jnp.int32(0))
    arrived_ref[me] = message_ref[me]

    def rotate(source, width, begin, end):
        def step(i, carry):
            columns = pl.ds(pl.multiple_of(i * 256, 256), 256)
            turned = lax.dot_general(rotation_ref[:, columns], source[...], TT, preferred_element_type=F32)
            upper = turned.astype(BF)
            lower = (turned - upper.astype(F32)).astype(BF)
            turned_ref[pl.ds(i * 16, 16), 0:DS, 0:width] = upper.reshape(16, DS, width)
            turned_ref[pl.ds(i * 16, 16), DS : 2 * DS, 0:width] = lower.reshape(16, DS, width)
            return carry

        lax.fori_loop(begin, end, step, 0)

    def group(codes, g, width):
        level = levels(128, width)
        upper, lower = [], []
        for j in range(8):
            row = codes[pl.ds(g * 8 + j, 1), :]
            picked = onehot((row & 127).astype(F32).astype(BF), level)
            high = jnp.broadcast_to((row >> 7).astype(F32).astype(BF), (2 * DS, width))
            values = turned_ref[g * 8 + j, :, 0:width]
            zero = jnp.zeros_like(values)
            masked = jnp.concatenate(
                [jnp.where(high == jnp.asarray(0, BF), values, zero), jnp.where(high == jnp.asarray(1, BF), values, zero)],
                0,
            )
            both = lax.dot_general(masked, picked, NT, preferred_element_type=F32)
            lower.append(both[0:16] + both[16:32])
            upper.append(both[32:48] + both[48:64])
        return jnp.concatenate(lower, 0).T, jnp.concatenate(upper, 0).T

    loads[0].wait()
    loads[1].wait()

    def near_cross(i, carry):
        columns = pl.ds(pl.multiple_of(i * 256, 256), 256)
        block = lax.dot_general(vectors_ref[:, columns], near_reb_ref[...], TT, preferred_element_type=F32)
        cross_ref[i] = block.reshape(4, 2, 4, 8, D)
        return carry

    lax.fori_loop(0, 4, near_cross, 0)
    rotate(vectors_ref, NEAR, 0, 4)

    def near_total(g, carry):
        lower, upper = group(near_codes_ref, g, NEAR)
        total_ref[g % 2, 0:2, :, :, g // 2] = lower.reshape(2, 4, 2, 8, 128)
        total_ref[g % 2, 2:4, :, :, g // 2] = upper.reshape(2, 4, 2, 8, 128)
        return carry

    lax.fori_loop(0, 8, near_total, 0)

    def widen(i, carry):
        chunk_load(i).wait()

        def part(k, inner):
            source = chunk_ref.at[lax.rem(i, 2)]
            for c in range(8):
                piece = source[pl.ds(pl.multiple_of(k * 16, 16), 16), c * 128 : (c + 1) * 128].astype(F32)
                start = pl.multiple_of((i * (CHUNK // 16) + k) * 128 + c * 8, 8)
                table_ref[pl.ds(start, 8), :] = piece[0:8]
                table_ref[pl.ds(pl.multiple_of(start + 64, 8), 8), :] = piece[8:16]
            return inner

        lax.fori_loop(0, CHUNK // 16, part, 0)

        @pl.when(i + 2 < LISTS // CHUNK)
        def _():
            chunk_load(i + 2).start()

        return carry

    lax.fori_loop(0, LISTS // CHUNK, widen, 0)
    table_ref[LISTS * 8 : LISTS * 8 + 64, :] = jnp.zeros((64, 128), F32)

    drain(arrived_ref.at[pl.ds(0, DEVICES - 1)], message_recv)
    for i in range(8):
        arrived_wide_ref[i * 256 : (i + 1) * 256] = arrived_ref[i * 16 : (i + 1) * 16].astype(F32).reshape(256, 128)
    for j in range(CAP):
        turned_over = arrived_wide_ref[pl.ds(j, DEVICES, stride=SLOT), :].T.astype(I32) - 1
        far_codes_ref[:, j * 128 : (j + 1) * 128] = turned_over[0:M]
        upper, lower = turned_over[M : M + 1], turned_over[M + 1 : M + 2]
        row = jnp.clip(jnp.where(upper < 0, LISTS, upper * 64 + lower), 0, LISTS)
        row_ref[j : j + 1, :] = (row >> 3) * 64 + (row & 7)
    for j in range(CAP, 16):
        row_ref[j : j + 1, :] = jnp.zeros((1, 128), I32)
    counted = jnp.sum(arrived_wide_ref[pl.ds(CAP, DEVICES, stride=SLOT), :], axis=0, keepdims=True)
    fetch = pltpu.make_async_copy(row_ref, row_smem, local_sem.at[2])
    fetch.start()

    def far_decode(i, carry):
        for block in range(CAP):
            span = slice(block * 128, (block + 1) * 128)
            decode(lambda m, span=span: far_codes_ref[pl.ds(m, 1), :][:, span], far_reb_ref, i, span)
        return carry

    lax.fori_loop(0, M // 8, far_decode, 0)
    fetch.wait()

    def gather(j, carry):
        def take(k, inner):
            pieces = [table_ref[pl.ds(row_smem[j, k * 16 + s], 8, stride=8), :] for s in range(16)]
            for s in range(16):
                stage_ref[pl.ds(k * 128 + (s // 8) * 64 + s % 8, 8, stride=8), :] = pieces[s]
            return inner

        lax.fori_loop(0, 8, take, 0)
        block = stage_ref[...].reshape(16, 8, 8, 128)
        for c in range(8):
            far_x_ref[pl.ds(pl.multiple_of(j * 128, 128), 128), c * 128 : (c + 1) * 128] = (
                -block[:, c].reshape(128, 128)
            ).astype(BF)
        return carry

    lax.fori_loop(0, CAP, gather, 0)

    def slab(q):
        return lax.rem(x + 1 + q, 4)

    def cross_core(q):
        return remote(
            cross_ref.at[slab(q), :, 1 - core],
            cross_half_ref.at[slab(q)],
            cross_core_send.at[q],
            cross_core_recv.at[q],
            mate,
        )

    def lanes(p):
        return slice(PARTS[p][0], PARTS[p][1])

    def over_x(q):
        i = slab(q)
        return remote(
            cross_half_ref.at[i, :, :, :, lanes(0)], over_x_ref.at[q], over_x_send.at[q], over_x_recv.at[q], device(x=i)
        )

    def over_y(q, s):
        i, j = slab(q), lax.rem(y + s, 4)
        return remote(
            cross_half_ref.at[i, :, j, :, lanes(1)],
            over_y_ref.at[s - 1, i],
            over_y_send.at[q, s - 1],
            over_y_recv.at[q, s - 1],
            device(y=j),
        )

    def over_z(q, s):
        i, j = slab(q), lax.rem(z + s, 4)
        return remote(
            cross_half_ref.at[i, j, :, :, lanes(2)],
            over_z_ref.at[s - 1, i],
            over_z_send.at[q, s - 1],
            over_z_recv.at[q, s - 1],
            device(z=j),
        )

    def join(q):
        cross_core(q).wait_recv()
        cross_half_ref[slab(q)] += cross_ref[slab(q), :, core]
        for s in range(1, 4):
            over_y(q, s).start()
            over_z(q, s).start()

    def far_cross(q, carry):
        i = slab(q)
        columns = pl.ds(pl.multiple_of(i * 256, 256), 256)
        block = lax.dot_general(far_x_ref[:, columns], far_reb_ref[...], TT, preferred_element_type=F32)
        cross_ref[i] += block.reshape(4, 2, 4, 8, D)
        cross_core(q).start()

        @pl.when(q >= 2)
        def _():
            join(q - 2)
            over_x(q - 2).start()

        return carry

    lax.fori_loop(0, 4, far_cross, 0)
    rotate(far_x_ref, FAR, 0, 1)
    join(2)
    over_x(2).start()
    rotate(far_x_ref, FAR, 1, 2)
    join(3)
    rotate(far_x_ref, FAR, 2, 4)

    def side(q):
        return lax.rem(y + 1 + q, 4)

    def total_core(q, half):
        return remote(
            total_ref.at[half, :, :, 1 - core, side(q)],
            total_half_ref.at[q, half],
            total_core_send.at[q, half],
            total_core_recv.at[q, half],
            mate,
        )

    def total_side(q):
        return remote(
            total_half_ref.at[q],
            total_side_ref.at[q],
            total_side_send.at[q],
            total_side_recv.at[q],
            (r, side(q)),
        )

    def far_total(q, begin, end):
        def step(half, carry):
            lower, upper = group(far_codes_ref, side(q) * 2 + half, FAR)
            total_ref[half, 0:2, :, :, side(q)] += lower.reshape(2, 4, 2, 8, 128)
            total_ref[half, 2:4, :, :, side(q)] += upper.reshape(2, 4, 2, 8, 128)
            total_core(q, half).start(0)
            return carry

        lax.fori_loop(begin, end, step, 0)

    def pass_on(q):
        for half in range(2):
            total_core(q, half).wait_recv()
        total_half_ref[q] += total_ref[:, :, :, core, side(q)]
        if q < 3:
            total_side(q).start(0)

    def spread(start):
        for j in range(1, 4):
            start(0, j)

        def row(i, carry):
            for j in range(4):
                start(i, j)
            return carry

        lax.fori_loop(1, 4, row, 0)

    def cross_plane(p, di, dj):
        axes = PARTS[p][3]
        i, j = lax.rem(at[axes[0]] + di, 4), lax.rem(at[axes[1]] + dj, 4)
        remote(
            cross_plane_ref.at[i, j, :, lanes(p)],
            cross_got_ref.at[di * 4 + dj, :, lanes(p)],
            cross_plane_send.at[p],
            cross_plane_recv.at[p],
            device(**{axes[0]: i, axes[1]: j}),
        ).start()

    far_total(0, 0, 2)
    far_total(1, 0, 1)
    pass_on(0)
    far_total(1, 1, 2)
    far_total(2, 0, 1)
    pass_on(1)
    far_total(2, 1, 2)

    far_total(3, 0, 1)
    pass_on(2)
    far_total(3, 1, 2)
    for q in range(3):
        over_x(q).wait_recv()
    cross_plane_ref[:, :, :, lanes(0)] = (
        cross_half_ref[x, :, :, :, lanes(0)] + over_x_ref[0] + over_x_ref[1] + over_x_ref[2]
    )
    spread(lambda di, dj: cross_plane(0, di, dj))

    def arrived_over(q, carry):
        for s in range(1, 4):
            over_y(q, s).wait_recv()
            over_z(q, s).wait_recv()
        return carry

    lax.fori_loop(0, 4, arrived_over, 0)
    cross_plane_ref[:, :, :, lanes(1)] = (
        cross_half_ref[:, :, y, :, lanes(1)] + over_y_ref[0] + over_y_ref[1] + over_y_ref[2]
    )
    spread(lambda di, dj: cross_plane(1, di, dj))
    cross_plane_ref[:, :, :, lanes(2)] = (
        cross_half_ref[:, z, :, :, lanes(2)] + over_z_ref[0] + over_z_ref[1] + over_z_ref[2]
    )
    spread(lambda di, dj: cross_plane(2, di, dj))
    pass_on(3)
    for q in range(3):
        total_side(q).wait_recv()
    total_plane_ref[...] = total_half_ref[3] + total_side_ref[0] + total_side_ref[1] + total_side_ref[2]

    def total_plane(di, dj):
        i, j = lax.rem(x + di, 4), lax.rem(z + dj, 4)
        remote(
            total_plane_ref.at[:, i, j],
            total_got_ref.at[di * 4 + dj],
            total_plane_send,
            total_plane_recv,
            device(x=i, z=j),
        ).start(0)

    spread(total_plane)
    for p in range(3):
        axes = PARTS[p][3]
        drain(cross_got_ref.at[pl.ds(1, 15), :, lanes(p)], cross_plane_recv.at[p])
        acc = cross_plane_ref[at[axes[0]], at[axes[1]], :, lanes(p)]
        for step in range(1, 16):
            acc = acc + cross_got_ref[step, :, lanes(p)]
        out_cross_ref[:, lanes(p)] = acc
    drain(total_got_ref.at[pl.ds(1, 15)], total_plane_recv)
    for half in range(2):
        acc = total_plane_ref[half, x, z]
        for step in range(1, 16):
            acc = acc + total_got_ref[step, half]
        out_total_ref[half] = acc
    out_counts_ref[...] = jnp.broadcast_to(counted, (8, 128))

    drain(message_ref.at[pl.ds(0, DEVICES - 1)], message_send)

    def left(q, carry):
        cross_core(q).wait_send()
        for s in range(1, 4):
            over_y(q, s).wait_send()
            over_z(q, s).wait_send()
        return carry

    lax.fori_loop(0, 4, left, 0)
    for p in range(3):
        over_x(p).wait_send()
        drain(cross_got_ref.at[pl.ds(1, 15), :, lanes(p)], cross_plane_send.at[p])
    for q in range(4):
        for half in range(2):
            total_core(q, half).wait_send()
        if q < 3:
            total_side(q).wait_send()
    drain(total_got_ref.at[pl.ds(1, 15)], total_plane_send)


def finish_kernel(total_ref, counts_ref, cross_ref, out_book_ref, out_cross_ref):
    out_cross_ref[...] = cross_ref[...] / jnp.sqrt(jnp.float32(NEAR * DEVICES))
    for half in range(2):
        where = (half * 8 + (iota((8, 128), 1) >> 4)) * 8 + iota((8, 128), 0)
        counts = jnp.take_along_axis(counts_ref[...], where, axis=1)
        mean = total_ref[half] / (counts + 1.0)
        for j in range(8):
            out_book_ref[half * 8 + j] = mean[:, j * DS : (j + 1) * DS]


def per_device(vectors, coarse_list, list_slot, codes, centroids, rotation, codebook):
    book = codebook.transpose(0, 2, 1).reshape(D, K)
    here = pl.BlockSpec(memory_space=VMEM)
    away = pl.BlockSpec(memory_space=ANY)
    total, counts, cross = pl.pallas_call(
        kernel,
        out_shape=(
            jax.ShapeDtypeStruct((2, 8, 128), F32),
            jax.ShapeDtypeStruct((8, 128), F32),
            jax.ShapeDtypeStruct((8, D), F32),
        ),
        in_specs=[pl.BlockSpec(memory_space=pltpu.SMEM), here, here, here, away, away, away, away],
        out_specs=(here, here, here),
        scratch_shapes=[
            VMEM((LISTS, 128), I32),
            VMEM((NEAR, 128), I32),
            VMEM((NEAR, D), BF),
            VMEM((D, D), BF),
            VMEM((2, CHUNK, D), BF),
            VMEM((LISTS * 8 + 64, 128), F32),
            VMEM((D, K), F32),
            VMEM((DEVICES, SLOT, 128), BF),
            VMEM((DEVICES, SLOT, 128), BF),
            VMEM((DEVICES * SLOT, 128), F32),
            VMEM((M, FAR), I32),
            VMEM((16, 128), I32),
            pltpu.SMEM((16, 128), I32),
            VMEM((128, 128), F32),
            VMEM((D, NEAR), BF),
            VMEM((D, FAR), BF),
            VMEM((1024, 128), F32),
            VMEM((FAR, D), BF),
            VMEM((M, 2 * DS, FAR), BF),
            VMEM((4, 4, 2, 4, 8, D), F32),
            VMEM((2, 4, 4, 2, 4, 8, 128), F32),
            VMEM((4, 4, 4, 8, D), F32),
            VMEM((3, 4, 4, 8, 384), F32),
            VMEM((3, 4, 4, 8, 256), F32),
            VMEM((3, 4, 4, 8, 384), F32),
            VMEM((4, 4, 8, D), F32),
            VMEM((16, 8, D), F32),
            VMEM((4, 2, 4, 4, 8, 128), F32),
            VMEM((3, 2, 4, 4, 8, 128), F32),
            VMEM((2, 4, 4, 8, 128), F32),
            VMEM((16, 2, 8, 128), F32),
            DMA((4,)),
            DMA((2,)),
            DMA,
            DMA,
            DMA((4,)),
            DMA((4,)),
            DMA((3,)),
            DMA((3,)),
            DMA((4, 3)),
            DMA((4, 3)),
            DMA((4, 3)),
            DMA((4, 3)),
            DMA((3,)),
            DMA((3,)),
            DMA((4, 2)),
            DMA((4, 2)),
            DMA((3,)),
            DMA((3,)),
            DMA,
            DMA,
        ],
        compiler_params=pltpu.CompilerParams(
            collective_id=0, has_side_effects=True, vmem_limit_bytes=56 * 2**20
        ),
        name="refine",
    )(
        coarse_list,
        coarse_list.reshape(1, NEAR),
        codes.T,
        book,
        list_slot.reshape(LISTS, 128),
        vectors,
        rotation,
        centroids,
    )
    return pl.pallas_call(
        finish_kernel,
        out_shape=(jax.ShapeDtypeStruct((16, 8, DS), F32), jax.ShapeDtypeStruct((8, D), F32)),
        in_specs=[here] * 3,
        out_specs=(here, here),
        name="finish",
    )(total, counts, cross)


def solution(mesh):
    placed = (
        P(("rows", "sub"), None),
        P(("rows", "sub")),
        P(),
        P(("rows", "sub"), None),
        P(("rows", "sub"), None),
        P(),
        P(),
    )
    return jax.shard_map(
        per_device,
        mesh=mesh,
        in_specs=placed,
        out_specs=(P("sub", "rows", None), P(("rows", "sub"), None)),
        check_vma=False,
    )
```

```python
import jax
import jax.numpy as jnp
from jax import lax
from jax.experimental import pallas as pl
from jax.experimental.pallas import tpu as pltpu
from jax.sharding import PartitionSpec as P

D = 1024
M = 64
K = 256
DS = 16
NEAR = 256
LISTS = 4096
DEVICES = 128
CAP = 10
SLOT = 16
FAR = CAP * DEVICES
CHUNK = 512
F32 = jnp.float32
BF = jnp.bfloat16
I32 = jnp.int32
MESH = pl.DeviceIdType.MESH
VMEM = pltpu.VMEM
ANY = pl.ANY
DMA = pltpu.SemaphoreType.DMA

PIECES = (("y", 0, 0, 256, 0), ("x", 1, 0, 256, 0), ("z", 2, 0, 256, 0), ("x", 3, 0, 128, 256), ("z", 3, 128, 256, 256))
WIDTH = {"x": 384, "y": 256, "z": 384}
PLANE = {"x": "zy", "y": "xz", "z": "xy"}
NT = (((1,), (1,)), ((), ()))
TT = (((0,), (1,)), ((), ()))


def onehot(row, level):
    return jnp.where(row == level, jnp.asarray(1, BF), jnp.asarray(0, BF))


def iota(shape, dim):
    return lax.broadcasted_iota(I32, shape, dim)


def levels(count, width):
    return iota((count, width), 0).astype(F32).astype(BF)


def drain(ref, semaphore):
    pltpu.make_async_copy(ref, ref, semaphore).wait()


def kernel(
    coarse_smem,
    coarse_ref,
    near_codes_ref,
    book_ref,
    slots_hbm,
    vectors_hbm,
    rotation_hbm,
    centroids_hbm,
    out_total_ref,
    out_counts_ref,
    out_cross_ref,
    slots_ref,
    picked_ref,
    vectors_ref,
    rotation_ref,
    chunk_ref,
    table_ref,
    table_book_ref,
    message_ref,
    arrived_ref,
    arrived_wide_ref,
    far_codes_ref,
    row_ref,
    row_smem,
    counts_ref,
    near_reb_ref,
    far_reb_ref,
    stage_ref,
    far_x_ref,
    turned_ref,
    cross_ref,
    total_ref,
    cross_half_ref,
    over_refs,
    near_xt_ref,
    plane_refs,
    got_refs,
    total_half_ref,
    total_side_ref,
    total_plane_ref,
    total_got_ref,
    local_sem,
    chunk_sem,
    message_send,
    message_recv,
    cross_core_send,
    cross_core_recv,
    piece_send,
    piece_recv,
    cross_plane_send,
    cross_plane_recv,
    total_core_send,
    total_core_recv,
    total_side_send,
    total_side_recv,
    total_plane_send,
    total_plane_recv,
):
    r, y = lax.axis_index("rows"), lax.axis_index("sub")
    core, z, x = lax.rem(r, 2), lax.rem(lax.div(r, 2), 4), lax.div(r, 8)
    me = r * 4 + y
    at = {"x": x, "y": y, "z": z}

    def device(**place):
        spot = dict(at, **place)
        return ((spot["x"] * 4 + spot["z"]) * 2 + core, spot["y"])

    mate = (r + 1 - 2 * core, y)

    def remote(source, target, send, recv, to):
        return pltpu.make_async_remote_copy(
            src_ref=source, dst_ref=target, send_sem=send, recv_sem=recv, device_id=to, device_id_type=MESH
        )

    def others(dr, first):
        there = lax.rem(r + dr, DEVICES // 4)
        return [(there, lax.rem(y + dy, 4)) for dy in range(first, 4)]

    barrier = pltpu.get_barrier_semaphore()

    def greet(dr, first):
        for other in others(dr, first):
            pl.semaphore_signal(barrier, inc=1, device_id=other, device_id_type=MESH)

    loads = [
        pltpu.make_async_copy(vectors_hbm, vectors_ref, local_sem.at[0]),
        pltpu.make_async_copy(rotation_hbm, rotation_ref, local_sem.at[1]),
    ]
    slots_load = pltpu.make_async_copy(slots_hbm, slots_ref, local_sem.at[3])
    slots_load.start()

    level32, level128 = levels(32, NEAR), levels(128, NEAR)
    counts_ref[...] = jnp.zeros((128, 128), F32)

    def count(i):
        acc = jnp.zeros((32, 128), F32)
        for j in range(8):
            m = i * 8 + j
            row = near_codes_ref[pl.ds(m, 1), :]
            upper = onehot((row >> 3).astype(F32).astype(BF), level32)
            lower = onehot(((row & 7) + 8 * lax.rem(m, 16)).astype(F32).astype(BF), level128)
            acc = acc + lax.dot_general(upper, lower, NT, preferred_element_type=F32)
        counts_ref[pl.ds(pl.multiple_of(lax.div(i, 2) * 32, 32), 32), :] += acc

    def greet_and_count(i, carry):
        for k in range(4):
            greet(i * 4 + k, 0)
        count(i)
        return carry

    for k in range(4):
        greet(k, 1 if k == 0 else 0)
    count(jnp.int32(0))
    lax.fori_loop(1, 8, greet_and_count, 0)
    for i in range(8):
        rows = pl.ds(i * 128, 128)
        table_book_ref[rows, :] = book_ref[rows, :].astype(F32)

    slots_load.wait()
    for load in loads:
        load.start()

    def chunk_load(i):
        return pltpu.make_async_copy(
            centroids_hbm.at[pl.ds(i * CHUNK, CHUNK)], chunk_ref.at[lax.rem(i, 2)], chunk_sem.at[lax.rem(i, 2)]
        )

    chunk_load(0).start()
    chunk_load(1).start()

    def look_up(i, carry):
        for s in range(16):
            line = coarse_smem[i * 16 + s] >> 7
            picked_ref[pl.ds(i * 16 + s, 1), :] = slots_ref[pl.ds(line, 1), :]
        return carry

    lax.fori_loop(0, NEAR // 16, look_up, 0)
    coarse = jnp.broadcast_to(coarse_ref[...].astype(F32), (128, NEAR)).T.astype(I32)
    mine = iota((NEAR, 128), 1) == (coarse & 127)
    slot = jnp.sum(jnp.where(mine, picked_ref[...].astype(F32), 0.0), axis=1, keepdims=True)
    down = jnp.broadcast_to(slot, (NEAR, NEAR))
    along = down.T.astype(I32)
    down = down.astype(I32)

    owner = along >> 12
    same = (owner == (down >> 12)) & (iota((NEAR, NEAR), 0) < iota((NEAR, NEAR), 1))
    rank = jnp.sum(jnp.where(same, 1, 0), axis=0, keepdims=True)
    position = owner[0:1] * SLOT + rank
    local_row = along[0:M] & (LISTS - 1)
    line = iota((M, NEAR), 0)
    digits = jnp.where(line == 0, (local_row >> 6) + 1, jnp.where(line == 1, (local_row & 63) + 1, 0))
    tokens = jnp.concatenate([near_codes_ref[...] + 1, digits], axis=0).astype(F32).T
    column = iota((1, 128), 1)
    count_position = ((column & 31) * 4 + (column >> 5)) * SLOT + CAP
    place_of = jnp.concatenate([position, count_position], axis=1)
    payload = jnp.concatenate([tokens.astype(BF), counts_ref[...].astype(BF)], axis=0)

    def build(i, carry):
        place = jnp.where(iota((256, NEAR + 128), 0) + i * 256 == place_of, 1.0, 0.0).astype(BF)
        rows = jnp.dot(place, payload, preferred_element_type=F32)
        message_ref[pl.ds(i * 16, 16)] = rows.astype(BF).reshape(16, SLOT, 128)
        return carry

    lax.fori_loop(0, DEVICES * SLOT // 256, build, 0)
    pl.semaphore_wait(barrier, DEVICES - 1)

    def post(dr, first):
        for other in others(dr, first):
            remote(
                message_ref.at[other[0] * 4 + other[1]], arrived_ref.at[me], message_send, message_recv, other
            ).start()

    def decode(codes, target, i, span, count=8):
        for j in range(count):
            m = i * count + j
            index = jnp.broadcast_to(codes(m), (8, 128))
            low, high = index & 127, index >= 128
            halves = []
            for half in range(2):
                start = pl.multiple_of(m * DS + 8 * half, 8)
                first = jnp.take_along_axis(table_book_ref[pl.ds(start, 8), 0:128], low, axis=1)
                second = jnp.take_along_axis(table_book_ref[pl.ds(start, 8), 128:256], low, axis=1)
                halves.append(jnp.where(high, second, first))
            target[pl.ds(pl.multiple_of(m * DS, DS), DS), span] = jnp.concatenate(halves, 0).astype(BF)

    def near_decode(i):
        for block in range(NEAR // 128):
            span = slice(block * 128, (block + 1) * 128)
            decode(lambda m, span=span: near_codes_ref[pl.ds(m, 1), :][:, span], near_reb_ref, i, span)

    def post_and_decode(i, carry):
        for k in range(4):
            post(i * 4 + k, 0)
        near_decode(i)
        return carry

    for k in range(4):
        post(k, 1 if k == 0 else 0)
    lax.fori_loop(1, 8, post_and_decode, 0)
    near_decode(jnp.int32(0))
    arrived_ref[me] = message_ref[me]

    def rotate(source, width, begin, end):
        def step(i, carry):
            columns = pl.ds(pl.multiple_of(i * 256, 256), 256)
            turned = lax.dot_general(rotation_ref[:, columns], source[...], TT, preferred_element_type=F32)
            upper = turned.astype(BF)
            lower = (turned - upper.astype(F32)).astype(BF)
            turned_ref[pl.ds(i * 16, 16), 0:DS, 0:width] = upper.reshape(16, DS, width)
            turned_ref[pl.ds(i * 16, 16), DS : 2 * DS, 0:width] = lower.reshape(16, DS, width)
            return carry

        lax.fori_loop(begin, end, step, 0)

    def group(codes, g, width):
        level = levels(128, width)
        upper, lower = [], []
        for j in range(8):
            row = codes[pl.ds(g * 8 + j, 1), :]
            picked = onehot((row & 127).astype(F32).astype(BF), level)
            high = jnp.broadcast_to((row >> 7).astype(F32).astype(BF), (2 * DS, width))
            values = turned_ref[g * 8 + j, :, 0:width]
            zero = jnp.zeros_like(values)
            masked = jnp.concatenate(
                [jnp.where(high == jnp.asarray(0, BF), values, zero), jnp.where(high == jnp.asarray(1, BF), values, zero)],
                0,
            )
            both = lax.dot_general(masked, picked, NT, preferred_element_type=F32)
            lower.append(both[0:16] + both[16:32])
            upper.append(both[32:48] + both[48:64])
        return jnp.concatenate(lower, 0).T, jnp.concatenate(upper, 0).T

    loads[0].wait()
    loads[1].wait()

    for i in range(8):
        near_xt_ref[i * 128 : (i + 1) * 128, :] = vectors_ref[:, i * 128 : (i + 1) * 128].T

    def near_cross(q, carry):
        rows = near_reb_ref[pl.ds(pl.multiple_of(q * 256, 256), 256), :]
        for i in range(4):
            block = lax.dot_general(near_xt_ref[i * 256 : (i + 1) * 256, :], rows, NT, preferred_element_type=F32)
            cross_ref[q, i] = block.reshape(4, 2, 4, 8, 256)
        return carry

    lax.fori_loop(0, 4, near_cross, 0)
    rotate(vectors_ref, NEAR, 0, 4)

    def near_total(g, carry):
        lower, upper = group(near_codes_ref, g, NEAR)
        total_ref[g % 2, 0:2, :, :, g // 2] = lower.reshape(2, 4, 2, 8, 128)
        total_ref[g % 2, 2:4, :, :, g // 2] = upper.reshape(2, 4, 2, 8, 128)
        return carry

    lax.fori_loop(0, 8, near_total, 0)

    def widen(i, carry):
        chunk_load(i).wait()

        def part(kk, inner):
            source = chunk_ref.at[lax.rem(i, 2)]
            for k in range(4):
                for c in range(8):
                    first = pl.multiple_of(kk * 64 + k * 16, 16)
                    piece = source[pl.ds(first, 16), c * 128 : (c + 1) * 128].astype(F32)
                    start = pl.multiple_of((i * (CHUNK // 64) + kk) * 512 + k * 128 + c * 8, 8)
                    table_ref[pl.ds(start, 8), :] = piece[0:8]
                    table_ref[pl.ds(pl.multiple_of(start + 64, 8), 8), :] = piece[8:16]
            return inner

        lax.fori_loop(0, CHUNK // 64, part, 0)

        @pl.when(i + 2 < LISTS // CHUNK)
        def _():
            chunk_load(i + 2).start()

        return carry

    lax.fori_loop(0, LISTS // CHUNK, widen, 0)
    table_ref[LISTS * 8 : LISTS * 8 + 64, :] = jnp.zeros((64, 128), F32)

    drain(arrived_ref.at[pl.ds(0, DEVICES - 1)], message_recv)
    for i in range(8):
        arrived_wide_ref[i * 256 : (i + 1) * 256] = arrived_ref[i * 16 : (i + 1) * 16].astype(F32).reshape(256, 128)
    for j in range(CAP):
        turned_over = arrived_wide_ref[pl.ds(j, DEVICES, stride=SLOT), :].T.astype(I32) - 1
        far_codes_ref[:, j * 128 : (j + 1) * 128] = turned_over[0:M]
        upper, lower = turned_over[M : M + 1], turned_over[M + 1 : M + 2]
        row = jnp.clip(jnp.where(upper < 0, LISTS, upper * 64 + lower), 0, LISTS)
        row_ref[j : j + 1, :] = (row >> 3) * 64 + (row & 7)
    for j in range(CAP, 16):
        row_ref[j : j + 1, :] = jnp.zeros((1, 128), I32)
    counted = jnp.sum(arrived_wide_ref[pl.ds(CAP, DEVICES, stride=SLOT), :], axis=0, keepdims=True)
    fetch = pltpu.make_async_copy(row_ref, row_smem, local_sem.at[2])
    fetch.start()

    def far_decode(q, i):
        for block in range(CAP):
            span = slice(block * 128, (block + 1) * 128)
            decode(lambda m, span=span: far_codes_ref[pl.ds(m, 1), :][:, span], far_reb_ref, q * 4 + i, span, 4)

    def first_decode(i, carry):
        far_decode(0, i)
        return carry

    lax.fori_loop(0, 4, first_decode, 0)
    fetch.wait()

    def gather(j, carry):
        def take(k, inner):
            for part in range(2):
                pieces = [table_ref[pl.ds(row_smem[j, k * 32 + part * 16 + s], 8, stride=8), :] for s in range(16)]
                for s in range(16):
                    start = k * 256 + part * 128 + (s // 8) * 64 + s % 8
                    stage_ref[pl.ds(start, 8, stride=8), :] = pieces[s]
            return inner

        lax.fori_loop(0, 4, take, 0)
        for c in range(8):
            for half in range(8):
                block = [stage_ref[k * 64 + c * 8 : k * 64 + c * 8 + 8, :] for k in (half * 2, half * 2 + 1)]
                start = pl.multiple_of(j * 128 + half * 16, 16)
                far_x_ref[pl.ds(start, 16), c * 128 : (c + 1) * 128] = (-jnp.concatenate(block, 0)).astype(BF)
        return carry

    lax.fori_loop(0, CAP, gather, 0)

    def cross_core(q):
        return remote(
            cross_ref.at[q, :, :, 1 - core],
            cross_half_ref.at[q],
            cross_core_send.at[q],
            cross_core_recv.at[q],
            mate,
        )

    def along_axis(axis, value):
        return tuple(value if d == axis else slice(None) for d in "xzy")

    def piece(k, step):
        axis, q, begin, end, offset = PIECES[k]
        there = lax.rem(at[axis] + step, 4)
        return remote(
            cross_half_ref.at[(q,) + along_axis(axis, there) + (slice(None), slice(begin, end))],
            over_refs[axis].at[step - 1, :, :, :, offset : offset + end - begin],
            piece_send.at[k, step - 1],
            piece_recv.at[k, step - 1],
            device(**{axis: there}),
        )

    def join(q):
        cross_core(q).wait_recv()
        cross_half_ref[q] += cross_ref[q, :, :, core]
        for k in range(5):
            if PIECES[k][1] == q:
                for step in range(1, 4):
                    piece(k, step).start()

    def far_cross(q):
        def step(i, carry):
            columns = pl.ds(pl.multiple_of(i * 256, 256), 256)
            rows = slice(q * 256, (q + 1) * 256)
            block = jnp.dot(far_reb_ref[rows, :], far_x_ref[:, columns], preferred_element_type=F32)
            if q < 3:
                far_decode(q + 1, i)
            cross_ref[q, i] += block.T.reshape(4, 2, 4, 8, 256)
            return carry

        lax.fori_loop(0, 4, step, 0)

    for q in range(4):
        far_cross(q)
        cross_core(q).start()
        if q >= 2:
            join(q - 2)
    rotate(far_x_ref, FAR, 0, 1)
    join(2)
    rotate(far_x_ref, FAR, 1, 2)
    join(3)
    rotate(far_x_ref, FAR, 2, 4)

    def side(q):
        return lax.rem(y + (2, 1, 3, 0)[q], 4)

    def total_core(q, half):
        return remote(
            total_ref.at[half, :, :, 1 - core, side(q)],
            total_half_ref.at[q, half],
            total_core_send.at[q, half],
            total_core_recv.at[q, half],
            mate,
        )

    def total_side(q, half):
        return remote(
            total_half_ref.at[q, half],
            total_side_ref.at[q, half],
            total_side_send.at[q, half],
            total_side_recv.at[q, half],
            (r, side(q)),
        )

    def far_total(q, half):
        def step(g, carry):
            lower, upper = group(far_codes_ref, g, FAR)
            total_ref[half, 0:2, :, :, side(q)] += lower.reshape(2, 4, 2, 8, 128)
            total_ref[half, 2:4, :, :, side(q)] += upper.reshape(2, 4, 2, 8, 128)
            return carry

        lax.fori_loop(side(q) * 2 + half, side(q) * 2 + half + 1, step, 0)
        total_core(q, half).start()

    def pass_on(q, half):
        total_core(q, half).wait_recv()
        total_half_ref[q, half] += total_ref[half, :, :, core, side(q)]
        if q < 3:
            total_side(q, half).start()

    def spread(start):
        for j in range(1, 4):
            start(0, j)

        def row(i, carry):
            for j in range(4):
                start(i, j)
            return carry

        lax.fori_loop(1, 4, row, 0)

    def cross_plane(axis, di, dj):
        axes = PLANE[axis]
        i, j = lax.rem(at[axes[0]] + di, 4), lax.rem(at[axes[1]] + dj, 4)
        remote(
            plane_refs[axis].at[i, j],
            got_refs[axis].at[di * 4 + dj],
            cross_plane_send.at["xyz".index(axis)],
            cross_plane_recv.at["xyz".index(axis)],
            device(**{axes[0]: i, axes[1]: j}),
        ).start()

    def over(axis):
        for k in range(5):
            name, q, begin, end, offset = PIECES[k]
            if name == axis:
                for step in range(1, 4):
                    piece(k, step).wait_recv()
                own = cross_half_ref[(q,) + along_axis(axis, at[axis]) + (slice(None), slice(begin, end))]
                place = slice(offset, offset + end - begin)
                got = over_refs[axis]
                plane_refs[axis][:, :, :, place] = (
                    own + got[0, :, :, :, place] + got[1, :, :, :, place] + got[2, :, :, :, place]
                )
        spread(lambda di, dj: cross_plane(axis, di, dj))

    for h in range(8):
        far_total(h // 2, h % 2)
        if h >= 1:
            pass_on((h - 1) // 2, (h - 1) % 2)
    over("y")
    over("x")
    over("z")
    pass_on(3, 1)
    for q in range(3):
        for half in range(2):
            total_side(q, half).wait_recv()
    total_plane_ref[...] = total_half_ref[3] + total_side_ref[0] + total_side_ref[1] + total_side_ref[2]

    def total_plane(di, dj):
        i, j = lax.rem(x + di, 4), lax.rem(z + dj, 4)
        remote(
            total_plane_ref.at[:, i, j],
            total_got_ref.at[di * 4 + dj],
            total_plane_send,
            total_plane_recv,
            device(x=i, z=j),
        ).start()

    spread(total_plane)
    for axis in "yxz":
        axes = PLANE[axis]
        drain(got_refs[axis].at[pl.ds(1, 15)], cross_plane_recv.at["xyz".index(axis)])
        acc = plane_refs[axis][at[axes[0]], at[axes[1]]]
        for step in range(1, 16):
            acc = acc + got_refs[axis][step]
        for name, q, begin, end, offset in PIECES:
            if name == axis:
                out_cross_ref[:, q * 256 + begin : q * 256 + end] = acc[:, offset : offset + end - begin]
    drain(total_got_ref.at[pl.ds(1, 15)], total_plane_recv)
    for half in range(2):
        acc = total_plane_ref[half, x, z]
        for step in range(1, 16):
            acc = acc + total_got_ref[step, half]
        out_total_ref[half] = acc
    out_counts_ref[...] = jnp.broadcast_to(counted, (8, 128))

    drain(message_ref.at[pl.ds(0, DEVICES - 1)], message_send)

    for q in range(4):
        cross_core(q).wait_send()
    for k in range(5):
        for step in range(1, 4):
            piece(k, step).wait_send()
    for axis in "xyz":
        drain(got_refs[axis].at[pl.ds(1, 15)], cross_plane_send.at["xyz".index(axis)])
    for q in range(4):
        for half in range(2):
            total_core(q, half).wait_send()
            if q < 3:
                total_side(q, half).wait_send()
    drain(total_got_ref.at[pl.ds(1, 15)], total_plane_send)


def finish_kernel(total_ref, counts_ref, cross_ref, out_book_ref, out_cross_ref):
    out_cross_ref[...] = cross_ref[...] / jnp.sqrt(jnp.float32(NEAR * DEVICES))
    for half in range(2):
        where = (half * 8 + (iota((8, 128), 1) >> 4)) * 8 + iota((8, 128), 0)
        counts = jnp.take_along_axis(counts_ref[...], where, axis=1)
        mean = total_ref[half] / (counts + 1.0)
        for j in range(8):
            out_book_ref[half * 8 + j] = mean[:, j * DS : (j + 1) * DS]


def per_device(vectors, coarse_list, list_slot, codes, centroids, rotation, codebook):
    book = codebook.transpose(0, 2, 1).reshape(D, K)
    here = pl.BlockSpec(memory_space=VMEM)
    away = pl.BlockSpec(memory_space=ANY)
    total, counts, cross = pl.pallas_call(
        kernel,
        out_shape=(
            jax.ShapeDtypeStruct((2, 8, 128), F32),
            jax.ShapeDtypeStruct((8, 128), F32),
            jax.ShapeDtypeStruct((8, D), F32),
        ),
        in_specs=[pl.BlockSpec(memory_space=pltpu.SMEM), here, here, here, away, away, away, away],
        out_specs=(here, here, here),
        scratch_shapes=[
            VMEM((LISTS, 128), I32),
            VMEM((NEAR, 128), I32),
            VMEM((NEAR, D), BF),
            VMEM((D, D), BF),
            VMEM((2, CHUNK, D), BF),
            VMEM((LISTS * 8 + 64, 128), F32),
            VMEM((D, K), F32),
            VMEM((DEVICES, SLOT, 128), BF),
            VMEM((DEVICES, SLOT, 128), BF),
            VMEM((DEVICES * SLOT, 128), F32),
            VMEM((M, FAR), I32),
            VMEM((16, 128), I32),
            pltpu.SMEM((16, 128), I32),
            VMEM((128, 128), F32),
            VMEM((D, NEAR), BF),
            VMEM((D, FAR), BF),
            VMEM((1024, 128), F32),
            VMEM((FAR, D), BF),
            VMEM((M, 2 * DS, FAR), BF),
            VMEM((4, 4, 4, 2, 4, 8, 256), F32),
            VMEM((2, 4, 4, 2, 4, 8, 128), F32),
            VMEM((4, 4, 4, 4, 8, 256), F32),
            {axis: VMEM((3, 4, 4, 8, width), F32) for axis, width in WIDTH.items()},
            VMEM((D, NEAR), BF),
            {axis: VMEM((4, 4, 8, width), F32) for axis, width in WIDTH.items()},
            {axis: VMEM((16, 8, width), F32) for axis, width in WIDTH.items()},
            VMEM((4, 2, 4, 4, 8, 128), F32),
            VMEM((3, 2, 4, 4, 8, 128), F32),
            VMEM((2, 4, 4, 8, 128), F32),
            VMEM((16, 2, 8, 128), F32),
            DMA((4,)),
            DMA((2,)),
            DMA,
            DMA,
            DMA((4,)),
            DMA((4,)),
            DMA((5, 3)),
            DMA((5, 3)),
            DMA((3,)),
            DMA((3,)),
            DMA((4, 2)),
            DMA((4, 2)),
            DMA((3, 2)),
            DMA((3, 2)),
            DMA,
            DMA,
        ],
        compiler_params=pltpu.CompilerParams(
            collective_id=0, has_side_effects=True, vmem_limit_bytes=56 * 2**20
        ),
        name="refine",
    )(
        coarse_list,
        coarse_list.reshape(1, NEAR),
        codes.T,
        book,
        list_slot.reshape(LISTS, 128),
        vectors,
        rotation,
        centroids,
    )
    return pl.pallas_call(
        finish_kernel,
        out_shape=(jax.ShapeDtypeStruct((16, 8, DS), F32), jax.ShapeDtypeStruct((8, D), F32)),
        in_specs=[here] * 3,
        out_specs=(here, here),
        name="finish",
    )(total, counts, cross)


def solution(mesh):
    placed = (
        P(("rows", "sub"), None),
        P(("rows", "sub")),
        P(),
        P(("rows", "sub"), None),
        P(("rows", "sub"), None),
        P(),
        P(),
    )
    return jax.shard_map(
        per_device,
        mesh=mesh,
        in_specs=placed,
        out_specs=(P("sub", "rows", None), P(("rows", "sub"), None)),
        check_vma=False,
    )
```

```python
import jax
import jax.numpy as jnp
from jax import lax
from jax.experimental import pallas as pl
from jax.experimental.pallas import tpu as pltpu
from jax.sharding import PartitionSpec as P

D = 1024
M = 64
K = 256
DS = 16
NEAR = 256
LISTS = 4096
DEVICES = 128
CAP = 10
SLOT = 16
FAR = CAP * DEVICES
CHUNK = 512
F32 = jnp.float32
BF = jnp.bfloat16
I32 = jnp.int32
MESH = pl.DeviceIdType.MESH
VMEM = pltpu.VMEM
ANY = pl.ANY
DMA = pltpu.SemaphoreType.DMA

PIECES = (("y", 0, 0, 256, 0), ("x", 1, 0, 256, 0), ("z", 2, 0, 256, 0), ("x", 3, 0, 128, 256), ("z", 3, 128, 256, 256))
WIDTH = {"x": 384, "y": 256, "z": 384}
PLANE = {"x": "zy", "y": "xz", "z": "xy"}
NT = (((1,), (1,)), ((), ()))
TT = (((0,), (1,)), ((), ()))


def onehot(row, level):
    return jnp.where(row == level, jnp.asarray(1, BF), jnp.asarray(0, BF))


def iota(shape, dim):
    return lax.broadcasted_iota(I32, shape, dim)


def levels(count, width):
    return iota((count, width), 0).astype(F32).astype(BF)


def drain(ref, semaphore):
    pltpu.make_async_copy(ref, ref, semaphore).wait()


def kernel(
    coarse_smem,
    coarse_ref,
    near_codes_ref,
    book_ref,
    slots_hbm,
    vectors_hbm,
    rotation_hbm,
    centroids_hbm,
    out_total_ref,
    out_counts_ref,
    out_cross_ref,
    slots_ref,
    picked_ref,
    vectors_ref,
    rotation_ref,
    chunk_ref,
    table_ref,
    table_book_ref,
    message_ref,
    arrived_ref,
    arrived_wide_ref,
    far_codes_ref,
    row_ref,
    row_smem,
    counts_ref,
    near_reb_ref,
    far_reb_ref,
    stage_ref,
    far_x_ref,
    turned_ref,
    cross_ref,
    total_ref,
    cross_half_ref,
    over_refs,
    near_xt_ref,
    plane_refs,
    got_refs,
    total_half_ref,
    total_side_ref,
    total_plane_ref,
    total_got_ref,
    local_sem,
    chunk_sem,
    message_send,
    message_recv,
    cross_core_send,
    cross_core_recv,
    piece_send,
    piece_recv,
    cross_plane_send,
    cross_plane_recv,
    total_core_send,
    total_core_recv,
    total_side_send,
    total_side_recv,
    total_plane_send,
    total_plane_recv,
):
    r, y = lax.axis_index("rows"), lax.axis_index("sub")
    core, z, x = lax.rem(r, 2), lax.rem(lax.div(r, 2), 4), lax.div(r, 8)
    me = r * 4 + y
    at = {"x": x, "y": y, "z": z}

    def device(**place):
        spot = dict(at, **place)
        return ((spot["x"] * 4 + spot["z"]) * 2 + core, spot["y"])

    mate = (r + 1 - 2 * core, y)

    def remote(source, target, send, recv, to):
        return pltpu.make_async_remote_copy(
            src_ref=source, dst_ref=target, send_sem=send, recv_sem=recv, device_id=to, device_id_type=MESH
        )

    def others(dr, first):
        there = lax.rem(r + dr, DEVICES // 4)
        return [(there, lax.rem(y + dy, 4)) for dy in range(first, 4)]

    barrier = pltpu.get_barrier_semaphore()

    def greet(dr, first):
        for other in others(dr, first):
            pl.semaphore_signal(barrier, inc=1, device_id=other, device_id_type=MESH)

    loads = [
        pltpu.make_async_copy(vectors_hbm, vectors_ref, local_sem.at[0]),
        pltpu.make_async_copy(rotation_hbm, rotation_ref, local_sem.at[1]),
    ]
    slots_load = pltpu.make_async_copy(slots_hbm, slots_ref, local_sem.at[3])
    slots_load.start()

    level32, level128 = levels(32, NEAR), levels(128, NEAR)
    counts_ref[...] = jnp.zeros((128, 128), F32)

    def count(i):
        acc = jnp.zeros((32, 128), F32)
        for j in range(8):
            m = i * 8 + j
            row = near_codes_ref[pl.ds(m, 1), :]
            upper = onehot((row >> 3).astype(F32).astype(BF), level32)
            lower = onehot(((row & 7) + 8 * lax.rem(m, 16)).astype(F32).astype(BF), level128)
            acc = acc + lax.dot_general(upper, lower, NT, preferred_element_type=F32)
        counts_ref[pl.ds(pl.multiple_of(lax.div(i, 2) * 32, 32), 32), :] += acc

    def greet_rows(i, carry):
        for k in range(4):
            greet(i * 4 + k, 0)
        return carry

    def count_step(i, carry):
        count(i * 2)
        count(i * 2 + 1)
        return carry

    for k in range(4):
        greet(k, 1 if k == 0 else 0)
    lax.fori_loop(1, 8, greet_rows, 0)
    lax.fori_loop(0, 4, count_step, 0)
    for i in range(8):
        rows = pl.ds(i * 128, 128)
        table_book_ref[rows, :] = book_ref[rows, :].astype(F32)

    slots_load.wait()
    for load in loads:
        load.start()

    def chunk_load(i):
        return pltpu.make_async_copy(
            centroids_hbm.at[pl.ds(i * CHUNK, CHUNK)], chunk_ref.at[lax.rem(i, 2)], chunk_sem.at[lax.rem(i, 2)]
        )

    chunk_load(0).start()
    chunk_load(1).start()

    def look_up(i, carry):
        for s in range(16):
            line = coarse_smem[i * 16 + s] >> 7
            picked_ref[pl.ds(i * 16 + s, 1), :] = slots_ref[pl.ds(line, 1), :]
        return carry

    lax.fori_loop(0, NEAR // 16, look_up, 0)
    coarse = jnp.broadcast_to(coarse_ref[...].astype(F32), (128, NEAR)).T.astype(I32)
    mine = iota((NEAR, 128), 1) == (coarse & 127)
    slot = jnp.sum(jnp.where(mine, picked_ref[...].astype(F32), 0.0), axis=1, keepdims=True)
    down = jnp.broadcast_to(slot, (NEAR, NEAR))
    along = down.T.astype(I32)
    down = down.astype(I32)

    owner = along >> 12
    same = (owner == (down >> 12)) & (iota((NEAR, NEAR), 0) < iota((NEAR, NEAR), 1))
    rank = jnp.sum(jnp.where(same, 1, 0), axis=0, keepdims=True)
    position = owner[0:1] * SLOT + rank
    local_row = along[0:M] & (LISTS - 1)
    line = iota((M, NEAR), 0)
    digits = jnp.where(line == 0, (local_row >> 6) + 1, jnp.where(line == 1, (local_row & 63) + 1, 0))
    tokens = jnp.concatenate([near_codes_ref[...] + 1, digits], axis=0).astype(F32).T
    column = iota((1, 128), 1)
    count_position = ((column & 31) * 4 + (column >> 5)) * SLOT + CAP
    place_of = jnp.concatenate([position, count_position], axis=1)
    payload = jnp.concatenate([tokens.astype(BF), counts_ref[...].astype(BF)], axis=0)

    def build(i, carry):
        place = jnp.where(iota((256, NEAR + 128), 0) + i * 256 == place_of, 1.0, 0.0).astype(BF)
        rows = jnp.dot(place, payload, preferred_element_type=F32)
        message_ref[pl.ds(i * 16, 16)] = rows.astype(BF).reshape(16, SLOT, 128)
        return carry

    lax.fori_loop(0, DEVICES * SLOT // 256, build, 0)
    pl.semaphore_wait(barrier, DEVICES - 1)

    def post(dr, first):
        for other in others(dr, first):
            remote(
                message_ref.at[other[0] * 4 + other[1]], arrived_ref.at[me], message_send, message_recv, other
            ).start()

    def decode(codes, target, i, span, count=8):
        for j in range(count):
            m = i * count + j
            index = jnp.broadcast_to(codes(m), (8, 128))
            low, high = index & 127, index >= 128
            halves = []
            for half in range(2):
                start = pl.multiple_of(m * DS + 8 * half, 8)
                first = jnp.take_along_axis(table_book_ref[pl.ds(start, 8), 0:128], low, axis=1)
                second = jnp.take_along_axis(table_book_ref[pl.ds(start, 8), 128:256], low, axis=1)
                halves.append(jnp.where(high, second, first))
            target[pl.ds(pl.multiple_of(m * DS, DS), DS), span] = jnp.concatenate(halves, 0).astype(BF)

    def near_decode(i):
        for block in range(NEAR // 128):
            span = slice(block * 128, (block + 1) * 128)
            decode(lambda m, span=span: near_codes_ref[pl.ds(m, 1), :][:, span], near_reb_ref, i, span)

    def post_and_decode(i, carry):
        for k in range(4):
            post(i * 4 + k, 0)
        near_decode(i)
        return carry

    for k in range(4):
        post(k, 1 if k == 0 else 0)
    lax.fori_loop(1, 8, post_and_decode, 0)
    near_decode(jnp.int32(0))
    arrived_ref[me] = message_ref[me]

    def rotate(source, width, begin, end):
        def step(i, carry):
            columns = pl.ds(pl.multiple_of(i * 256, 256), 256)
            turned = lax.dot_general(rotation_ref[:, columns], source[...], TT, preferred_element_type=F32)
            upper = turned.astype(BF)
            lower = (turned - upper.astype(F32)).astype(BF)
            turned_ref[pl.ds(i * 16, 16), 0:DS, 0:width] = upper.reshape(16, DS, width)
            turned_ref[pl.ds(i * 16, 16), DS : 2 * DS, 0:width] = lower.reshape(16, DS, width)
            return carry

        lax.fori_loop(begin, end, step, 0)

    def group(codes, g, width):
        level = levels(128, width)
        upper, lower = [], []
        for j in range(8):
            row = codes[pl.ds(g * 8 + j, 1), :]
            picked = onehot((row & 127).astype(F32).astype(BF), level)
            high = jnp.broadcast_to((row >> 7).astype(F32).astype(BF), (2 * DS, width))
            values = turned_ref[g * 8 + j, :, 0:width]
            zero = jnp.zeros_like(values)
            masked = jnp.concatenate(
                [jnp.where(high == jnp.asarray(0, BF), values, zero), jnp.where(high == jnp.asarray(1, BF), values, zero)],
                0,
            )
            both = lax.dot_general(masked, picked, NT, preferred_element_type=F32)
            lower.append(both[0:16] + both[16:32])
            upper.append(both[32:48] + both[48:64])
        return jnp.concatenate(lower, 0).T, jnp.concatenate(upper, 0).T

    loads[0].wait()
    loads[1].wait()

    for i in range(8):
        near_xt_ref[i * 128 : (i + 1) * 128, :] = vectors_ref[:, i * 128 : (i + 1) * 128].T

    def near_cross(h, carry):
        for k in range(2):
            q = h * 2 + k
            rows = near_reb_ref[pl.ds(pl.multiple_of(q * 256, 256), 256), :]
            for i in range(4):
                block = lax.dot_general(near_xt_ref[i * 256 : (i + 1) * 256, :], rows, NT, preferred_element_type=F32)
                cross_ref[q, i] = block.reshape(4, 2, 4, 8, 256)
        return carry

    lax.fori_loop(0, 2, near_cross, 0)
    rotate(vectors_ref, NEAR, 0, 4)

    def near_total(i, carry):
        for half in range(2):
            lower, upper = group(near_codes_ref, i * 2 + half, NEAR)
            total_ref[half, 0:2, :, :, i] = lower.reshape(2, 4, 2, 8, 128)
            total_ref[half, 2:4, :, :, i] = upper.reshape(2, 4, 2, 8, 128)
        return carry

    lax.fori_loop(0, 4, near_total, 0)

    def widen(i, carry):
        chunk_load(i).wait()

        def part(kk, inner):
            source = chunk_ref.at[lax.rem(i, 2)]
            for k in range(4):
                for c in range(8):
                    first = pl.multiple_of(kk * 64 + k * 16, 16)
                    piece = source[pl.ds(first, 16), c * 128 : (c + 1) * 128].astype(F32)
                    start = pl.multiple_of((i * (CHUNK // 64) + kk) * 512 + k * 128 + c * 8, 8)
                    table_ref[pl.ds(start, 8), :] = piece[0:8]
                    table_ref[pl.ds(pl.multiple_of(start + 64, 8), 8), :] = piece[8:16]
            return inner

        lax.fori_loop(0, CHUNK // 64, part, 0)

        @pl.when(i + 2 < LISTS // CHUNK)
        def _():
            chunk_load(i + 2).start()

        return carry

    lax.fori_loop(0, LISTS // CHUNK, widen, 0)
    table_ref[LISTS * 8 : LISTS * 8 + 64, :] = jnp.zeros((64, 128), F32)

    drain(arrived_ref.at[pl.ds(0, DEVICES - 1)], message_recv)
    for i in range(8):
        arrived_wide_ref[i * 256 : (i + 1) * 256] = arrived_ref[i * 16 : (i + 1) * 16].astype(F32).reshape(256, 128)
    for j in range(CAP):
        turned_over = arrived_wide_ref[pl.ds(j, DEVICES, stride=SLOT), :].T.astype(I32) - 1
        far_codes_ref[:, j * 128 : (j + 1) * 128] = turned_over[0:M]
        upper, lower = turned_over[M : M + 1], turned_over[M + 1 : M + 2]
        row = jnp.clip(jnp.where(upper < 0, LISTS, upper * 64 + lower), 0, LISTS)
        row_ref[j : j + 1, :] = (row >> 3) * 64 + (row & 7)
    for j in range(CAP, 16):
        row_ref[j : j + 1, :] = jnp.zeros((1, 128), I32)
    counted = jnp.sum(arrived_wide_ref[pl.ds(CAP, DEVICES, stride=SLOT), :], axis=0, keepdims=True)
    fetch = pltpu.make_async_copy(row_ref, row_smem, local_sem.at[2])
    fetch.start()

    def far_decode(q, i):
        for block in range(CAP):
            span = slice(block * 128, (block + 1) * 128)
            decode(lambda m, span=span: far_codes_ref[pl.ds(m, 1), :][:, span], far_reb_ref, q * 4 + i, span, 4)

    def first_decode(i, carry):
        far_decode(0, i)
        return carry

    lax.fori_loop(0, 4, first_decode, 0)
    fetch.wait()

    def gather(j, carry):
        def take(k, inner):
            for part in range(2):
                pieces = [table_ref[pl.ds(row_smem[j, k * 32 + part * 16 + s], 8, stride=8), :] for s in range(16)]
                for s in range(16):
                    start = k * 256 + part * 128 + (s // 8) * 64 + s % 8
                    stage_ref[pl.ds(start, 8, stride=8), :] = pieces[s]
            return inner

        lax.fori_loop(0, 4, take, 0)
        for c in range(8):
            for half in range(8):
                block = [stage_ref[k * 64 + c * 8 : k * 64 + c * 8 + 8, :] for k in (half * 2, half * 2 + 1)]
                start = pl.multiple_of(j * 128 + half * 16, 16)
                far_x_ref[pl.ds(start, 16), c * 128 : (c + 1) * 128] = (-jnp.concatenate(block, 0)).astype(BF)
        return carry

    lax.fori_loop(0, CAP, gather, 0)

    def cross_core(q):
        return remote(
            cross_ref.at[q, :, :, 1 - core],
            cross_half_ref.at[q],
            cross_core_send.at[q],
            cross_core_recv.at[q],
            mate,
        )

    def along_axis(axis, value):
        return tuple(value if d == axis else slice(None) for d in "xzy")

    def piece(k, step):
        axis, q, begin, end, offset = PIECES[k]
        there = lax.rem(at[axis] + step, 4)
        return remote(
            cross_half_ref.at[(q,) + along_axis(axis, there) + (slice(None), slice(begin, end))],
            over_refs[axis].at[step - 1, :, :, :, offset : offset + end - begin],
            piece_send.at[k, step - 1],
            piece_recv.at[k, step - 1],
            device(**{axis: there}),
        )

    def join(q):
        cross_core(q).wait_recv()
        cross_half_ref[q] += cross_ref[q, :, :, core]
        for k in range(5):
            if PIECES[k][1] == q:
                for step in range(1, 4):
                    piece(k, step).start()

    def far_cross(q):
        def step(i, carry):
            columns = pl.ds(pl.multiple_of(i * 256, 256), 256)
            rows = slice(q * 256, (q + 1) * 256)
            block = jnp.dot(far_reb_ref[rows, :], far_x_ref[:, columns], preferred_element_type=F32)
            if q < 3:
                far_decode(q + 1, i)
            cross_ref[q, i] += block.T.reshape(4, 2, 4, 8, 256)
            return carry

        lax.fori_loop(0, 4, step, 0)

    for q in range(4):
        far_cross(q)
        cross_core(q).start()
        if q >= 2:
            join(q - 2)
    rotate(far_x_ref, FAR, 0, 1)
    join(2)
    rotate(far_x_ref, FAR, 1, 2)
    join(3)
    rotate(far_x_ref, FAR, 2, 4)

    def side(q):
        return lax.rem(y + (2, 1, 3, 0)[q], 4)

    def total_core(q, half):
        return remote(
            total_ref.at[half, :, :, 1 - core, side(q)],
            total_half_ref.at[q, half],
            total_core_send.at[q, half],
            total_core_recv.at[q, half],
            mate,
        )

    def total_side(q, half):
        return remote(
            total_half_ref.at[q, half],
            total_side_ref.at[q, half],
            total_side_send.at[q, half],
            total_side_recv.at[q, half],
            (r, side(q)),
        )

    def far_total(q, half):
        def step(g, carry):
            lower, upper = group(far_codes_ref, g, FAR)
            total_ref[half, 0:2, :, :, side(q)] += lower.reshape(2, 4, 2, 8, 128)
            total_ref[half, 2:4, :, :, side(q)] += upper.reshape(2, 4, 2, 8, 128)
            return carry

        lax.fori_loop(side(q) * 2 + half, side(q) * 2 + half + 1, step, 0)
        total_core(q, half).start()

    def pass_on(q, half):
        total_core(q, half).wait_recv()
        total_half_ref[q, half] += total_ref[half, :, :, core, side(q)]
        if q < 3:
            total_side(q, half).start()

    def spread(start):
        for j in range(1, 4):
            start(0, j)

        def row(i, carry):
            for j in range(4):
                start(i, j)
            return carry

        lax.fori_loop(1, 4, row, 0)

    def cross_plane(axis, di, dj):
        axes = PLANE[axis]
        i, j = lax.rem(at[axes[0]] + di, 4), lax.rem(at[axes[1]] + dj, 4)
        remote(
            plane_refs[axis].at[i, j],
            got_refs[axis].at[di * 4 + dj],
            cross_plane_send.at["xyz".index(axis)],
            cross_plane_recv.at["xyz".index(axis)],
            device(**{axes[0]: i, axes[1]: j}),
        ).start()

    def over(axis):
        for k in range(5):
            name, q, begin, end, offset = PIECES[k]
            if name == axis:
                for step in range(1, 4):
                    piece(k, step).wait_recv()
                own = cross_half_ref[(q,) + along_axis(axis, at[axis]) + (slice(None), slice(begin, end))]
                place = slice(offset, offset + end - begin)
                got = over_refs[axis]
                plane_refs[axis][:, :, :, place] = (
                    own + got[0, :, :, :, place] + got[1, :, :, :, place] + got[2, :, :, :, place]
                )
        spread(lambda di, dj: cross_plane(axis, di, dj))

    for h in range(8):
        far_total(h // 2, h % 2)
        if h >= 1:
            pass_on((h - 1) // 2, (h - 1) % 2)
    over("y")
    over("x")
    over("z")
    pass_on(3, 1)
    for q in range(3):
        for half in range(2):
            total_side(q, half).wait_recv()
    total_plane_ref[...] = total_half_ref[3] + total_side_ref[0] + total_side_ref[1] + total_side_ref[2]

    def total_plane(di, dj):
        i, j = lax.rem(x + di, 4), lax.rem(z + dj, 4)
        remote(
            total_plane_ref.at[:, i, j],
            total_got_ref.at[di * 4 + dj],
            total_plane_send,
            total_plane_recv,
            device(x=i, z=j),
        ).start()

    spread(total_plane)
    for axis in "yxz":
        axes = PLANE[axis]
        drain(got_refs[axis].at[pl.ds(1, 15)], cross_plane_recv.at["xyz".index(axis)])
        acc = plane_refs[axis][at[axes[0]], at[axes[1]]]
        for step in range(1, 16):
            acc = acc + got_refs[axis][step]
        for name, q, begin, end, offset in PIECES:
            if name == axis:
                out_cross_ref[:, q * 256 + begin : q * 256 + end] = acc[:, offset : offset + end - begin]
    drain(total_got_ref.at[pl.ds(1, 15)], total_plane_recv)
    for half in range(2):
        acc = total_plane_ref[half, x, z]
        for step in range(1, 16):
            acc = acc + total_got_ref[step, half]
        out_total_ref[half] = acc
    out_counts_ref[...] = jnp.broadcast_to(counted, (8, 128))

    drain(message_ref.at[pl.ds(0, DEVICES - 1)], message_send)

    for q in range(4):
        cross_core(q).wait_send()
    for k in range(5):
        for step in range(1, 4):
            piece(k, step).wait_send()
    for axis in "xyz":
        drain(got_refs[axis].at[pl.ds(1, 15)], cross_plane_send.at["xyz".index(axis)])
    for q in range(4):
        for half in range(2):
            total_core(q, half).wait_send()
            if q < 3:
                total_side(q, half).wait_send()
    drain(total_got_ref.at[pl.ds(1, 15)], total_plane_send)


def finish_kernel(total_ref, counts_ref, cross_ref, out_book_ref, out_cross_ref):
    out_cross_ref[...] = cross_ref[...] / jnp.sqrt(jnp.float32(NEAR * DEVICES))
    for half in range(2):
        where = (half * 8 + (iota((8, 128), 1) >> 4)) * 8 + iota((8, 128), 0)
        counts = jnp.take_along_axis(counts_ref[...], where, axis=1)
        mean = total_ref[half] / (counts + 1.0)
        for j in range(8):
            out_book_ref[half * 8 + j] = mean[:, j * DS : (j + 1) * DS]


def per_device(vectors, coarse_list, list_slot, codes, centroids, rotation, codebook):
    book = codebook.transpose(0, 2, 1).reshape(D, K)
    here = pl.BlockSpec(memory_space=VMEM)
    away = pl.BlockSpec(memory_space=ANY)
    total, counts, cross = pl.pallas_call(
        kernel,
        out_shape=(
            jax.ShapeDtypeStruct((2, 8, 128), F32),
            jax.ShapeDtypeStruct((8, 128), F32),
            jax.ShapeDtypeStruct((8, D), F32),
        ),
        in_specs=[pl.BlockSpec(memory_space=pltpu.SMEM), here, here, here, away, away, away, away],
        out_specs=(here, here, here),
        scratch_shapes=[
            VMEM((LISTS, 128), I32),
            VMEM((NEAR, 128), I32),
            VMEM((NEAR, D), BF),
            VMEM((D, D), BF),
            VMEM((2, CHUNK, D), BF),
            VMEM((LISTS * 8 + 64, 128), F32),
            VMEM((D, K), F32),
            VMEM((DEVICES, SLOT, 128), BF),
            VMEM((DEVICES, SLOT, 128), BF),
            VMEM((DEVICES * SLOT, 128), F32),
            VMEM((M, FAR), I32),
            VMEM((16, 128), I32),
            pltpu.SMEM((16, 128), I32),
            VMEM((128, 128), F32),
            VMEM((D, NEAR), BF),
            VMEM((D, FAR), BF),
            VMEM((1024, 128), F32),
            VMEM((FAR, D), BF),
            VMEM((M, 2 * DS, FAR), BF),
            VMEM((4, 4, 4, 2, 4, 8, 256), F32),
            VMEM((2, 4, 4, 2, 4, 8, 128), F32),
            VMEM((4, 4, 4, 4, 8, 256), F32),
            {axis: VMEM((3, 4, 4, 8, width), F32) for axis, width in WIDTH.items()},
            VMEM((D, NEAR), BF),
            {axis: VMEM((4, 4, 8, width), F32) for axis, width in WIDTH.items()},
            {axis: VMEM((16, 8, width), F32) for axis, width in WIDTH.items()},
            VMEM((4, 2, 4, 4, 8, 128), F32),
            VMEM((3, 2, 4, 4, 8, 128), F32),
            VMEM((2, 4, 4, 8, 128), F32),
            VMEM((16, 2, 8, 128), F32),
            DMA((4,)),
            DMA((2,)),
            DMA,
            DMA,
            DMA((4,)),
            DMA((4,)),
            DMA((5, 3)),
            DMA((5, 3)),
            DMA((3,)),
            DMA((3,)),
            DMA((4, 2)),
            DMA((4, 2)),
            DMA((3, 2)),
            DMA((3, 2)),
            DMA,
            DMA,
        ],
        compiler_params=pltpu.CompilerParams(
            collective_id=0, has_side_effects=True, vmem_limit_bytes=56 * 2**20
        ),
        name="refine",
    )(
        coarse_list,
        coarse_list.reshape(1, NEAR),
        codes.T,
        book,
        list_slot.reshape(LISTS, 128),
        vectors,
        rotation,
        centroids,
    )
    return pl.pallas_call(
        finish_kernel,
        out_shape=(jax.ShapeDtypeStruct((16, 8, DS), F32), jax.ShapeDtypeStruct((8, D), F32)),
        in_specs=[here] * 3,
        out_specs=(here, here),
        name="finish",
    )(total, counts, cross)


def solution(mesh):
    placed = (
        P(("rows", "sub"), None),
        P(("rows", "sub")),
        P(),
        P(("rows", "sub"), None),
        P(("rows", "sub"), None),
        P(),
        P(),
    )
    return jax.shard_map(
        per_device,
        mesh=mesh,
        in_specs=placed,
        out_specs=(P("sub", "rows", None), P(("rows", "sub"), None)),
        check_vma=False,
    )
```

```python
import jax
import jax.numpy as jnp
from jax import lax
from jax.experimental import pallas as pl
from jax.experimental.pallas import tpu as pltpu
from jax.sharding import PartitionSpec as P

D = 1024
M = 64
K = 256
DS = 16
NEAR = 256
LISTS = 4096
DEVICES = 128
CAP = 10
SLOT = 16
FAR = CAP * DEVICES
CHUNK = 512
F32 = jnp.float32
BF = jnp.bfloat16
I32 = jnp.int32
MESH = pl.DeviceIdType.MESH
VMEM = pltpu.VMEM
ANY = pl.ANY
DMA = pltpu.SemaphoreType.DMA

PIECES = (("y", 0, 0, 256, 0), ("x", 1, 0, 256, 0), ("z", 2, 0, 256, 0), ("x", 3, 0, 128, 256), ("z", 3, 128, 256, 256))
WIDTH = {"x": 384, "y": 256, "z": 384}
PLANE = {"x": "zy", "y": "xz", "z": "xy"}
NT = (((1,), (1,)), ((), ()))
TT = (((0,), (1,)), ((), ()))


def onehot(row, level):
    return jnp.where(row == level, jnp.asarray(1, BF), jnp.asarray(0, BF))


def iota(shape, dim):
    return lax.broadcasted_iota(I32, shape, dim)


def levels(count, width):
    return iota((count, width), 0).astype(F32).astype(BF)


def drain(ref, semaphore):
    pltpu.make_async_copy(ref, ref, semaphore).wait()


def kernel(
    coarse_smem,
    coarse_ref,
    near_codes_ref,
    book_ref,
    slots_hbm,
    vectors_hbm,
    rotation_hbm,
    centroids_hbm,
    out_total_ref,
    out_counts_ref,
    out_cross_ref,
    slots_ref,
    picked_ref,
    vectors_ref,
    rotation_ref,
    chunk_ref,
    table_ref,
    table_book_ref,
    message_ref,
    arrived_ref,
    arrived_wide_ref,
    far_codes_ref,
    row_ref,
    row_smem,
    counts_ref,
    near_reb_ref,
    far_reb_ref,
    stage_ref,
    far_x_ref,
    turned_ref,
    cross_ref,
    total_ref,
    cross_half_ref,
    over_refs,
    near_xt_ref,
    plane_refs,
    got_refs,
    total_half_ref,
    total_side_ref,
    total_plane_ref,
    total_got_ref,
    local_sem,
    chunk_sem,
    message_send,
    message_recv,
    cross_core_send,
    cross_core_recv,
    piece_send,
    piece_recv,
    cross_plane_send,
    cross_plane_recv,
    total_core_send,
    total_core_recv,
    total_side_send,
    total_side_recv,
    total_plane_send,
    total_plane_recv,
):
    r, y = lax.axis_index("rows"), lax.axis_index("sub")
    core, z, x = lax.rem(r, 2), lax.rem(lax.div(r, 2), 4), lax.div(r, 8)
    me = r * 4 + y
    at = {"x": x, "y": y, "z": z}

    def device(**place):
        spot = dict(at, **place)
        return ((spot["x"] * 4 + spot["z"]) * 2 + core, spot["y"])

    mate = (r + 1 - 2 * core, y)

    def remote(source, target, send, recv, to):
        return pltpu.make_async_remote_copy(
            src_ref=source, dst_ref=target, send_sem=send, recv_sem=recv, device_id=to, device_id_type=MESH
        )

    def others(dr, first):
        there = lax.rem(r + dr, DEVICES // 4)
        return [(there, lax.rem(y + dy, 4)) for dy in range(first, 4)]

    barrier = pltpu.get_barrier_semaphore()

    def greet(dr, first):
        for other in others(dr, first):
            pl.semaphore_signal(barrier, inc=1, device_id=other, device_id_type=MESH)

    loads = [
        pltpu.make_async_copy(vectors_hbm, vectors_ref, local_sem.at[0]),
        pltpu.make_async_copy(rotation_hbm, rotation_ref, local_sem.at[1]),
    ]
    slots_load = pltpu.make_async_copy(slots_hbm, slots_ref, local_sem.at[3])
    slots_load.start()

    level32, level128 = levels(32, NEAR), levels(128, NEAR)
    counts_ref[...] = jnp.zeros((128, 128), F32)

    def count(i):
        acc = jnp.zeros((32, 128), F32)
        for j in range(8):
            m = i * 8 + j
            row = near_codes_ref[pl.ds(m, 1), :]
            upper = onehot((row >> 3).astype(F32).astype(BF), level32)
            lower = onehot(((row & 7) + 8 * lax.rem(m, 16)).astype(F32).astype(BF), level128)
            acc = acc + lax.dot_general(upper, lower, NT, preferred_element_type=F32)
        counts_ref[pl.ds(pl.multiple_of(lax.div(i, 2) * 32, 32), 32), :] += acc

    def greet_rows(i, carry):
        for k in range(4):
            greet(i * 4 + k, 0)
        return carry

    def count_step(i, carry):
        count(i * 2)
        count(i * 2 + 1)
        return carry

    for k in range(4):
        greet(k, 1 if k == 0 else 0)
    lax.fori_loop(1, 8, greet_rows, 0)
    lax.fori_loop(0, 4, count_step, 0)
    slots_load.wait()
    for load in loads:
        load.start()

    def chunk_load(i):
        return pltpu.make_async_copy(
            centroids_hbm.at[pl.ds(i * CHUNK, CHUNK)], chunk_ref.at[lax.rem(i, 2)], chunk_sem.at[lax.rem(i, 2)]
        )

    chunk_load(0).start()
    chunk_load(1).start()

    def look_up(i, carry):
        for s in range(16):
            line = coarse_smem[i * 16 + s] >> 7
            picked_ref[pl.ds(i * 16 + s, 1), :] = slots_ref[pl.ds(line, 1), :]
        return carry

    lax.fori_loop(0, NEAR // 16, look_up, 0)
    coarse = jnp.broadcast_to(coarse_ref[...].astype(F32), (128, NEAR)).T.astype(I32)
    mine = iota((NEAR, 128), 1) == (coarse & 127)
    slot = jnp.sum(jnp.where(mine, picked_ref[...].astype(F32), 0.0), axis=1, keepdims=True)
    down = jnp.broadcast_to(slot, (NEAR, NEAR))
    along = down.T.astype(I32)
    down = down.astype(I32)

    owner = along >> 12
    same = (owner == (down >> 12)) & (iota((NEAR, NEAR), 0) < iota((NEAR, NEAR), 1))
    rank = jnp.sum(jnp.where(same, 1, 0), axis=0, keepdims=True)
    position = owner[0:1] * SLOT + rank
    local_row = along[0:M] & (LISTS - 1)
    line = iota((M, NEAR), 0)
    digits = jnp.where(line == 0, (local_row >> 6) + 1, jnp.where(line == 1, (local_row & 63) + 1, 0))
    tokens = jnp.concatenate([near_codes_ref[...] + 1, digits], axis=0).astype(F32).T
    column = iota((1, 128), 1)
    count_position = ((column & 31) * 4 + (column >> 5)) * SLOT + CAP
    place_of = jnp.concatenate([position, count_position], axis=1)
    payload = jnp.concatenate([tokens.astype(BF), counts_ref[...].astype(BF)], axis=0)

    def build(i, carry):
        place = jnp.where(iota((256, NEAR + 128), 0) + i * 256 == place_of, 1.0, 0.0).astype(BF)
        rows = jnp.dot(place, payload, preferred_element_type=F32)
        message_ref[pl.ds(i * 16, 16)] = rows.astype(BF).reshape(16, SLOT, 128)
        return carry

    lax.fori_loop(0, DEVICES * SLOT // 256, build, 0)
    pl.semaphore_wait(barrier, DEVICES - 1)

    def post(dr, first):
        for other in others(dr, first):
            remote(
                message_ref.at[other[0] * 4 + other[1]], arrived_ref.at[me], message_send, message_recv, other
            ).start()

    def decode(codes, target, i, span, count=8):
        for j in range(count):
            m = i * count + j
            index = jnp.broadcast_to(codes(m), (8, 128))
            low, high = index & 127, index >= 128
            halves = []
            for half in range(2):
                start = pl.multiple_of(m * DS + 8 * half, 8)
                first = jnp.take_along_axis(table_book_ref[pl.ds(start, 8), 0:128], low, axis=1)
                second = jnp.take_along_axis(table_book_ref[pl.ds(start, 8), 128:256], low, axis=1)
                halves.append(jnp.where(high, second, first))
            target[pl.ds(pl.multiple_of(m * DS, DS), DS), span] = jnp.concatenate(halves, 0).astype(BF)

    def near_decode(i):
        for block in range(NEAR // 128):
            span = slice(block * 128, (block + 1) * 128)
            decode(lambda m, span=span: near_codes_ref[pl.ds(m, 1), :][:, span], near_reb_ref, i, span)

    def post_and_decode(i, carry):
        for k in range(4):
            post(i * 4 + k, 0)
        near_decode(i)
        return carry

    for k in range(4):
        post(k, 1 if k == 0 else 0)
    for i in range(8):
        rows = pl.ds(i * 128, 128)
        table_book_ref[rows, :] = book_ref[rows, :].astype(F32)

    lax.fori_loop(1, 8, post_and_decode, 0)
    near_decode(jnp.int32(0))
    arrived_ref[me] = message_ref[me]

    def rotate(source, width, begin, end):
        def step(i, carry):
            columns = pl.ds(pl.multiple_of(i * 256, 256), 256)
            turned = lax.dot_general(rotation_ref[:, columns], source[...], TT, preferred_element_type=F32)
            upper = turned.astype(BF)
            lower = (turned - upper.astype(F32)).astype(BF)
            turned_ref[pl.ds(i * 16, 16), 0:DS, 0:width] = upper.reshape(16, DS, width)
            turned_ref[pl.ds(i * 16, 16), DS : 2 * DS, 0:width] = lower.reshape(16, DS, width)
            return carry

        lax.fori_loop(begin, end, step, 0)

    def group(codes, g, width):
        level = levels(128, width)
        upper, lower = [], []
        for j in range(8):
            row = codes[pl.ds(g * 8 + j, 1), :]
            picked = onehot((row & 127).astype(F32).astype(BF), level)
            high = jnp.broadcast_to((row >> 7).astype(F32).astype(BF), (2 * DS, width))
            values = turned_ref[g * 8 + j, :, 0:width]
            zero = jnp.zeros_like(values)
            masked = jnp.concatenate(
                [jnp.where(high == jnp.asarray(0, BF), values, zero), jnp.where(high == jnp.asarray(1, BF), values, zero)],
                0,
            )
            both = lax.dot_general(masked, picked, NT, preferred_element_type=F32)
            lower.append(both[0:16] + both[16:32])
            upper.append(both[32:48] + both[48:64])
        return jnp.concatenate(lower, 0).T, jnp.concatenate(upper, 0).T

    loads[0].wait()
    loads[1].wait()

    for i in range(8):
        near_xt_ref[i * 128 : (i + 1) * 128, :] = vectors_ref[:, i * 128 : (i + 1) * 128].T

    def near_cross(h, carry):
        for k in range(2):
            q = h * 2 + k
            rows = near_reb_ref[pl.ds(pl.multiple_of(q * 256, 256), 256), :]
            for i in range(4):
                block = lax.dot_general(near_xt_ref[i * 256 : (i + 1) * 256, :], rows, NT, preferred_element_type=F32)
                cross_ref[q, i] = block.reshape(4, 2, 4, 8, 256)
        return carry

    lax.fori_loop(0, 2, near_cross, 0)
    rotate(vectors_ref, NEAR, 0, 4)

    def near_total(i, carry):
        for half in range(2):
            lower, upper = group(near_codes_ref, i * 2 + half, NEAR)
            total_ref[half, 0:2, :, :, i] = lower.reshape(2, 4, 2, 8, 128)
            total_ref[half, 2:4, :, :, i] = upper.reshape(2, 4, 2, 8, 128)
        return carry

    lax.fori_loop(0, 4, near_total, 0)

    def widen(i, carry):
        chunk_load(i).wait()

        def part(kk, inner):
            source = chunk_ref.at[lax.rem(i, 2)]
            for k in range(4):
                for c in range(8):
                    first = pl.multiple_of(kk * 64 + k * 16, 16)
                    piece = source[pl.ds(first, 16), c * 128 : (c + 1) * 128].astype(F32)
                    start = pl.multiple_of((i * (CHUNK // 64) + kk) * 512 + k * 128 + c * 8, 8)
                    table_ref[pl.ds(start, 8), :] = piece[0:8]
                    table_ref[pl.ds(pl.multiple_of(start + 64, 8), 8), :] = piece[8:16]
            return inner

        lax.fori_loop(0, CHUNK // 64, part, 0)

        @pl.when(i + 2 < LISTS // CHUNK)
        def _():
            chunk_load(i + 2).start()

        return carry

    lax.fori_loop(0, LISTS // CHUNK, widen, 0)
    table_ref[LISTS * 8 : LISTS * 8 + 64, :] = jnp.zeros((64, 128), F32)

    drain(arrived_ref.at[pl.ds(0, DEVICES - 1)], message_recv)
    for i in range(8):
        arrived_wide_ref[i * 256 : (i + 1) * 256] = arrived_ref[i * 16 : (i + 1) * 16].astype(F32).reshape(256, 128)
    for j in range(CAP):
        turned_over = arrived_wide_ref[pl.ds(j, DEVICES, stride=SLOT), :].T.astype(I32) - 1
        far_codes_ref[:, j * 128 : (j + 1) * 128] = turned_over[0:M]
        upper, lower = turned_over[M : M + 1], turned_over[M + 1 : M + 2]
        row = jnp.clip(jnp.where(upper < 0, LISTS, upper * 64 + lower), 0, LISTS)
        row_ref[j : j + 1, :] = (row >> 3) * 64 + (row & 7)
    for j in range(CAP, 16):
        row_ref[j : j + 1, :] = jnp.zeros((1, 128), I32)
    counted = jnp.sum(arrived_wide_ref[pl.ds(CAP, DEVICES, stride=SLOT), :], axis=0, keepdims=True)
    fetch = pltpu.make_async_copy(row_ref, row_smem, local_sem.at[2])
    fetch.start()

    def far_decode(q, i):
        for block in range(CAP):
            span = slice(block * 128, (block + 1) * 128)
            decode(lambda m, span=span: far_codes_ref[pl.ds(m, 1), :][:, span], far_reb_ref, q * 4 + i, span, 4)

    def first_decode(i, carry):
        far_decode(0, i)
        return carry

    lax.fori_loop(0, 4, first_decode, 0)
    fetch.wait()

    def gather(j, carry):
        def take(k, inner):
            for part in range(2):
                pieces = [table_ref[pl.ds(row_smem[j, k * 32 + part * 16 + s], 8, stride=8), :] for s in range(16)]
                for s in range(16):
                    start = k * 256 + part * 128 + (s // 8) * 64 + s % 8
                    stage_ref[pl.ds(start, 8, stride=8), :] = pieces[s]
            return inner

        lax.fori_loop(0, 4, take, 0)
        for c in range(8):
            for half in range(8):
                block = [stage_ref[k * 64 + c * 8 : k * 64 + c * 8 + 8, :] for k in (half * 2, half * 2 + 1)]
                start = pl.multiple_of(j * 128 + half * 16, 16)
                far_x_ref[pl.ds(start, 16), c * 128 : (c + 1) * 128] = (-jnp.concatenate(block, 0)).astype(BF)
        return carry

    lax.fori_loop(0, CAP, gather, 0)

    def cross_core(q):
        return remote(
            cross_ref.at[q, :, :, 1 - core],
            cross_half_ref.at[q],
            cross_core_send.at[q],
            cross_core_recv.at[q],
            mate,
        )

    def along_axis(axis, value):
        return tuple(value if d == axis else slice(None) for d in "xzy")

    def piece(k, step):
        axis, q, begin, end, offset = PIECES[k]
        there = lax.rem(at[axis] + step, 4)
        return remote(
            cross_half_ref.at[(q,) + along_axis(axis, there) + (slice(None), slice(begin, end))],
            over_refs[axis].at[step - 1, :, :, :, offset : offset + end - begin],
            piece_send.at[k, step - 1],
            piece_recv.at[k, step - 1],
            device(**{axis: there}),
        )

    def join(q):
        cross_core(q).wait_recv()
        cross_half_ref[q] += cross_ref[q, :, :, core]
        for k in range(5):
            if PIECES[k][1] == q:
                for step in range(1, 4):
                    piece(k, step).start()

    def far_cross(q):
        def step(i, carry):
            columns = pl.ds(pl.multiple_of(i * 256, 256), 256)
            rows = slice(q * 256, (q + 1) * 256)
            block = jnp.dot(far_reb_ref[rows, :], far_x_ref[:, columns], preferred_element_type=F32)
            if q < 3:
                far_decode(q + 1, i)
            cross_ref[q, i] += block.T.reshape(4, 2, 4, 8, 256)
            return carry

        lax.fori_loop(0, 4, step, 0)

    for q in range(4):
        far_cross(q)
        cross_core(q).start()
        if q >= 2:
            join(q - 2)
    rotate(far_x_ref, FAR, 0, 1)
    join(2)
    rotate(far_x_ref, FAR, 1, 2)
    join(3)
    rotate(far_x_ref, FAR, 2, 4)

    def side(q):
        return lax.rem(y + (2, 1, 3, 0)[q], 4)

    def total_core(q, half):
        return remote(
            total_ref.at[half, :, :, 1 - core, side(q)],
            total_half_ref.at[q, half],
            total_core_send.at[q, half],
            total_core_recv.at[q, half],
            mate,
        )

    def total_side(q, half):
        return remote(
            total_half_ref.at[q, half],
            total_side_ref.at[q, half],
            total_side_send.at[q, half],
            total_side_recv.at[q, half],
            (r, side(q)),
        )

    def far_total(q, half):
        def step(g, carry):
            lower, upper = group(far_codes_ref, g, FAR)
            total_ref[half, 0:2, :, :, side(q)] += lower.reshape(2, 4, 2, 8, 128)
            total_ref[half, 2:4, :, :, side(q)] += upper.reshape(2, 4, 2, 8, 128)
            return carry

        lax.fori_loop(side(q) * 2 + half, side(q) * 2 + half + 1, step, 0)
        total_core(q, half).start()

    def pass_on(q, half):
        total_core(q, half).wait_recv()
        total_half_ref[q, half] += total_ref[half, :, :, core, side(q)]
        if q < 3:
            total_side(q, half).start()

    def spread(start):
        for j in range(1, 4):
            start(0, j)

        def row(i, carry):
            for j in range(4):
                start(i, j)
            return carry

        lax.fori_loop(1, 4, row, 0)

    def cross_plane(axis, di, dj):
        axes = PLANE[axis]
        i, j = lax.rem(at[axes[0]] + di, 4), lax.rem(at[axes[1]] + dj, 4)
        remote(
            plane_refs[axis].at[i, j],
            got_refs[axis].at[di * 4 + dj],
            cross_plane_send.at["xyz".index(axis)],
            cross_plane_recv.at["xyz".index(axis)],
            device(**{axes[0]: i, axes[1]: j}),
        ).start()

    def over(axis):
        for k in range(5):
            name, q, begin, end, offset = PIECES[k]
            if name == axis:
                for step in range(1, 4):
                    piece(k, step).wait_recv()
                own = cross_half_ref[(q,) + along_axis(axis, at[axis]) + (slice(None), slice(begin, end))]
                place = slice(offset, offset + end - begin)
                got = over_refs[axis]
                plane_refs[axis][:, :, :, place] = (
                    own + got[0, :, :, :, place] + got[1, :, :, :, place] + got[2, :, :, :, place]
                )
        spread(lambda di, dj: cross_plane(axis, di, dj))

    for h in range(8):
        far_total(h // 2, h % 2)
        if h >= 1:
            pass_on((h - 1) // 2, (h - 1) % 2)
    over("y")
    over("x")
    over("z")
    pass_on(3, 1)
    for q in range(3):
        for half in range(2):
            total_side(q, half).wait_recv()
    total_plane_ref[...] = total_half_ref[3] + total_side_ref[0] + total_side_ref[1] + total_side_ref[2]

    def total_plane(di, dj):
        i, j = lax.rem(x + di, 4), lax.rem(z + dj, 4)
        remote(
            total_plane_ref.at[:, i, j],
            total_got_ref.at[di * 4 + dj],
            total_plane_send,
            total_plane_recv,
            device(x=i, z=j),
        ).start()

    spread(total_plane)
    for axis in "yxz":
        axes = PLANE[axis]
        drain(got_refs[axis].at[pl.ds(1, 15)], cross_plane_recv.at["xyz".index(axis)])
        acc = plane_refs[axis][at[axes[0]], at[axes[1]]]
        for step in range(1, 16):
            acc = acc + got_refs[axis][step]
        for name, q, begin, end, offset in PIECES:
            if name == axis:
                out_cross_ref[:, q * 256 + begin : q * 256 + end] = acc[:, offset : offset + end - begin]
    drain(total_got_ref.at[pl.ds(1, 15)], total_plane_recv)
    for half in range(2):
        acc = total_plane_ref[half, x, z]
        for step in range(1, 16):
            acc = acc + total_got_ref[step, half]
        out_total_ref[half] = acc
    out_counts_ref[...] = jnp.broadcast_to(counted, (8, 128))

    drain(message_ref.at[pl.ds(0, DEVICES - 1)], message_send)

    for q in range(4):
        cross_core(q).wait_send()
    for k in range(5):
        for step in range(1, 4):
            piece(k, step).wait_send()
    for axis in "xyz":
        drain(got_refs[axis].at[pl.ds(1, 15)], cross_plane_send.at["xyz".index(axis)])
    for q in range(4):
        for half in range(2):
            total_core(q, half).wait_send()
            if q < 3:
                total_side(q, half).wait_send()
    drain(total_got_ref.at[pl.ds(1, 15)], total_plane_send)


def finish_kernel(total_ref, counts_ref, cross_ref, out_book_ref, out_cross_ref):
    out_cross_ref[...] = cross_ref[...] / jnp.sqrt(jnp.float32(NEAR * DEVICES))
    for half in range(2):
        where = (half * 8 + (iota((8, 128), 1) >> 4)) * 8 + iota((8, 128), 0)
        counts = jnp.take_along_axis(counts_ref[...], where, axis=1)
        mean = total_ref[half] / (counts + 1.0)
        for j in range(8):
            out_book_ref[half * 8 + j] = mean[:, j * DS : (j + 1) * DS]


def per_device(vectors, coarse_list, list_slot, codes, centroids, rotation, codebook):
    book = codebook.transpose(0, 2, 1).reshape(D, K)
    here = pl.BlockSpec(memory_space=VMEM)
    away = pl.BlockSpec(memory_space=ANY)
    total, counts, cross = pl.pallas_call(
        kernel,
        out_shape=(
            jax.ShapeDtypeStruct((2, 8, 128), F32),
            jax.ShapeDtypeStruct((8, 128), F32),
            jax.ShapeDtypeStruct((8, D), F32),
        ),
        in_specs=[pl.BlockSpec(memory_space=pltpu.SMEM), here, here, here, away, away, away, away],
        out_specs=(here, here, here),
        scratch_shapes=[
            VMEM((LISTS, 128), I32),
            VMEM((NEAR, 128), I32),
            VMEM((NEAR, D), BF),
            VMEM((D, D), BF),
            VMEM((2, CHUNK, D), BF),
            VMEM((LISTS * 8 + 64, 128), F32),
            VMEM((D, K), F32),
            VMEM((DEVICES, SLOT, 128), BF),
            VMEM((DEVICES, SLOT, 128), BF),
            VMEM((DEVICES * SLOT, 128), F32),
            VMEM((M, FAR), I32),
            VMEM((16, 128), I32),
            pltpu.SMEM((16, 128), I32),
            VMEM((128, 128), F32),
            VMEM((D, NEAR), BF),
            VMEM((D, FAR), BF),
            VMEM((1024, 128), F32),
            VMEM((FAR, D), BF),
            VMEM((M, 2 * DS, FAR), BF),
            VMEM((4, 4, 4, 2, 4, 8, 256), F32),
            VMEM((2, 4, 4, 2, 4, 8, 128), F32),
            VMEM((4, 4, 4, 4, 8, 256), F32),
            {axis: VMEM((3, 4, 4, 8, width), F32) for axis, width in WIDTH.items()},
            VMEM((D, NEAR), BF),
            {axis: VMEM((4, 4, 8, width), F32) for axis, width in WIDTH.items()},
            {axis: VMEM((16, 8, width), F32) for axis, width in WIDTH.items()},
            VMEM((4, 2, 4, 4, 8, 128), F32),
            VMEM((3, 2, 4, 4, 8, 128), F32),
            VMEM((2, 4, 4, 8, 128), F32),
            VMEM((16, 2, 8, 128), F32),
            DMA((4,)),
            DMA((2,)),
            DMA,
            DMA,
            DMA((4,)),
            DMA((4,)),
            DMA((5, 3)),
            DMA((5, 3)),
            DMA((3,)),
            DMA((3,)),
            DMA((4, 2)),
            DMA((4, 2)),
            DMA((3, 2)),
            DMA((3, 2)),
            DMA,
            DMA,
        ],
        compiler_params=pltpu.CompilerParams(
            collective_id=0, has_side_effects=True, vmem_limit_bytes=56 * 2**20
        ),
        name="refine",
    )(
        coarse_list,
        coarse_list.reshape(1, NEAR),
        codes.T,
        book,
        list_slot.reshape(LISTS, 128),
        vectors,
        rotation,
        centroids,
    )
    return pl.pallas_call(
        finish_kernel,
        out_shape=(jax.ShapeDtypeStruct((16, 8, DS), F32), jax.ShapeDtypeStruct((8, D), F32)),
        in_specs=[here] * 3,
        out_specs=(here, here),
        name="finish",
    )(total, counts, cross)


def solution(mesh):
    placed = (
        P(("rows", "sub"), None),
        P(("rows", "sub")),
        P(),
        P(("rows", "sub"), None),
        P(("rows", "sub"), None),
        P(),
        P(),
    )
    return jax.shard_map(
        per_device,
        mesh=mesh,
        in_specs=placed,
        out_specs=(P("sub", "rows", None), P(("rows", "sub"), None)),
        check_vma=False,
    )
```
